32 devices in a mesh: tm: 4 (over y, core), lon: 4 (over z), head: 2 (over x).
Axes of the slice: x: 2, y: 2, z: 4, core: 2. Of those that a mesh axis runs over, the one named last changes fastest.
Arguments:
- query_field: bfloat16 [48, 8, 32, 1536], P('tm', None, 'lon', 'head'), may hold values from -8 to 8
- key_field: bfloat16 [48, 8, 32, 1536], P('tm', None, 'lon', 'head'), may hold values from -8 to 8
- value_field: bfloat16 [48, 8, 32, 1536], P('tm', None, 'lon', 'head'), may hold values from -6 to 6
- tile_offsets: int32 [8, 4], P('tm', 'lon'), may hold values from -1 to 1
- timesteps: int32 [8], P('tm'), may hold values from 0 to 999
- gate_weight: float32 [256, 1536], P(None, 'head'), may hold values from -0.375 to 0.375
Outputs:
- gated_field: bfloat16 [48, 8, 32, 1536], P('tm', None, 'lon', 'head')
The draws below stay inside these ranges and needn't reach their ends.
Inputs may be any that keep to these rules, and one draw needn't show every extreme that they name: `tile_offsets`: the query tile (t, L) with shift s attends longitude tiles L + s - 1 to L + s + 1 around the loop.
All inputs are finite; a program needn't handle non-finite values.
Results may differ from the reference program's by a relative error of at most 0.0037.
Values may be sent and summed in bfloat16 or wider, within the bound.
A program may use at most 128 MiB of HBM per device.

```python
import math
import jax
import jax.numpy as jnp
from jax import lax

HEADS = 12
HD = 128
FREQ = 256
TILE_T = 6
TILE_H = 8
TILE_W = 8
NTT = 8
FRAMES = 48
COLS = 32
F = 1536
N_LON = 4


def draw_query_field(key, part):
    key = jax.random.fold_in(key, 11)
    base_key = jax.random.fold_in(key, 0)
    full_shape = (FRAMES, TILE_H, COLS, HEADS, HD)
    drawn = jnp.clip(jax.random.normal(base_key, full_shape, jnp.float32), -8.0, 8.0)
    return drawn.reshape(FRAMES, TILE_H, COLS, HEADS * HD).astype(jnp.bfloat16)


def draw_key_field(key, part):
    key = jax.random.fold_in(key, 23)
    base_key = jax.random.fold_in(key, 0)
    full_shape = (FRAMES, TILE_H, COLS, HEADS, HD)
    drawn = jnp.clip(2.0 * jax.random.normal(base_key, full_shape, jnp.float32), -8.0, 8.0)
    return drawn.reshape(FRAMES, TILE_H, COLS, HEADS * HD).astype(jnp.bfloat16)


def set_ends(result, rng, low, largest):
    extent = result.shape
    index_at = [jax.random.randint(jax.random.fold_in(rng, axis), (), 0, extent[axis]) for axis in range(len(extent))]
    result = result.at[tuple(index_at)].set(low)
    longest = extent.index(max(extent))
    index_at[longest] = (index_at[longest] + 1) % extent[longest]
    return result.at[tuple(index_at)].set(largest)


def block_scale(own_key, shape, cuts, low, largest):
    def one(position, blocks):
        draws = jax.random.uniform(jax.random.fold_in(jax.random.fold_in(own_key, 6), position), (blocks,), jnp.float32, low / len(cuts), largest / len(cuts))
        return jnp.repeat(jnp.exp(draws), shape[position] // blocks).reshape((-1,) + (1,) * (len(shape) - position - 1))

    loudness = one(*cuts[0])
    for cut in cuts[1:]:
        loudness = loudness * one(*cut)
    return loudness


def noise(own_key, shape, deviation, bound, cuts=(), kind=jnp.bfloat16):
    gain = block_scale(own_key, shape, cuts, -0.22, 0.18) if cuts else 1.0
    result = jax.random.normal(own_key, shape, jnp.float32) * deviation * gain
    return jnp.minimum(jnp.maximum(result, -bound), bound).astype(kind)


def setup_inputs(seed: int = 0) -> dict:
    key_of = jax.random.split(jax.random.key(seed), 7)
    query_field = draw_query_field(jax.random.fold_in(key_of[6], 71), 0)
    key_field = draw_key_field(jax.random.fold_in(key_of[6], 71), 0)
    value_field = noise(key_of[2], (FRAMES, TILE_H, COLS, F), 1.0, 6.0, ((0, 4), (2, 4), (3, 2)))
    tile_offsets = set_ends(jax.random.randint(key_of[3], (NTT, N_LON), -1, 2), jax.random.fold_in(key_of[3], 1), -1, 1).astype(jnp.int32)
    timesteps = set_ends(jax.random.randint(key_of[4], (NTT,), 0, 1000), jax.random.fold_in(key_of[4], 1), 0, 999).astype(jnp.int32)
    gate_weight = noise(key_of[5], (FREQ, F), FREQ ** -0.5, 0.375, ((1, 2),), jnp.float32)
    return dict(query_field=query_field, key_field=key_field, value_field=value_field, tile_offsets=tile_offsets, timesteps=timesteps, gate_weight=gate_weight)


def start_at(*entries):
    return tuple((jnp.asarray(entry).astype(jnp.int32) for entry in entries))

def reference(query_field, key_field, value_field, tile_offsets, timesteps, gate_weight):
    half_freq = FREQ // 2
    frequencies = jnp.exp(-math.log(10000.0) * jnp.arange(half_freq, dtype=jnp.float32) / half_freq)
    angles = timesteps.astype(jnp.float32)[:, None] * frequencies[None, :]
    embedding = jnp.concatenate([jnp.cos(angles), jnp.sin(angles)], axis=1)
    gate_rows = jnp.dot(embedding, gate_weight, precision=lax.Precision.HIGHEST, preferred_element_type=jnp.float32)
    lon_count = COLS // TILE_W
    tile_size = TILE_T * TILE_H * TILE_W
    keys_padded = jnp.pad(key_field, ((TILE_T, TILE_T), (0, 0), (0, 0), (0, 0)))
    values_padded = jnp.pad(value_field, ((TILE_T, TILE_T), (0, 0), (0, 0), (0, 0)))
    inv_root = 1.0 / math.sqrt(HD)

    def one_tile(tile_index):
        time_tile = (tile_index // lon_count).astype(jnp.int32)
        lon_tile = (tile_index % lon_count).astype(jnp.int32)
        lon_shift = tile_offsets[time_tile, lon_tile].astype(jnp.int32)
        query_rows = lax.dynamic_slice(query_field, start_at(time_tile * TILE_T, 0, lon_tile * TILE_W, 0), (TILE_T, TILE_H, TILE_W, F))
        query_rows = query_rows.reshape(tile_size, HEADS, HD).astype(jnp.float32)
        col_index = jnp.mod((lon_tile + lon_shift - 1) * TILE_W + jnp.arange(3 * TILE_W, dtype=jnp.int32), COLS).astype(jnp.int32)
        key_block = lax.dynamic_slice(keys_padded, start_at(time_tile * TILE_T, 0, 0, 0), (3 * TILE_T, TILE_H, COLS, F))
        value_block = lax.dynamic_slice(values_padded, start_at(time_tile * TILE_T, 0, 0, 0), (3 * TILE_T, TILE_H, COLS, F))
        key_block = jnp.take(key_block, col_index, axis=2).reshape(3, TILE_T * TILE_H * 3 * TILE_W, HEADS, HD).astype(jnp.float32)
        value_block = jnp.take(value_block, col_index, axis=2).reshape(3, TILE_T * TILE_H * 3 * TILE_W, HEADS, HD).astype(jnp.float32)
        window_times = time_tile - 1 + jnp.arange(3, dtype=jnp.int32)
        usable = (window_times >= 0) & (window_times < NTT)
        scores = jnp.einsum('qhd,jkhd->hqjk', query_rows, key_block) * inv_root
        scores = jnp.where(usable[None, None, :, None], scores, -1e+30)
        row_max = lax.optimization_barrier(jnp.max(scores, axis=(2, 3), keepdims=True))
        raised = jnp.exp(scores - row_max)
        totals = lax.optimization_barrier(jnp.sum(raised, axis=(2, 3)))
        weights = raised.astype(jnp.bfloat16)
        weighted = jnp.einsum('hqjk,jkhd->qhd', weights.astype(jnp.float32), value_block)
        gated = weighted / jnp.transpose(totals)[:, :, None] * gate_rows[time_tile].reshape(HEADS, HD)[None, :, :]
        return gated.astype(jnp.bfloat16)
    results = lax.map(one_tile, jnp.arange(NTT * lon_count, dtype=jnp.int32))
    results = results.reshape(NTT, lon_count, TILE_T, TILE_H, TILE_W, F)
    results = jnp.transpose(results, (0, 2, 3, 1, 4, 5))
    return results.reshape(FRAMES, TILE_H, COLS, F)
```

```python
import functools
import math

import jax
import jax.numpy as jnp
from jax import lax
from jax.experimental import pallas as pl
from jax.experimental.pallas import tpu as pltpu
from jax.sharding import PartitionSpec as P

HD = 128
FREQ = 256
TILE_T = 6
TILE_H = 8
TILE_W = 8
TILE = TILE_T * TILE_H * TILE_W
SCALE2 = math.log2(math.e) / math.sqrt(HD)
NEG = -1e30
CHUNK = 2
STATS = 8


def partial_kernel(times, columns, heads, flags_ref, q_ref, *refs):
    kv_refs = refs[: 3 * columns]
    o_ref, lse_ref, acc_ref, max_ref, stat_ref = refs[3 * columns :]
    head = pl.program_id(0)
    ones = jnp.ones((TILE, HD), jnp.bfloat16)
    lanes = lax.broadcasted_iota(jnp.int32, (TILE, HD), 1)
    prev_ok = flags_ref[columns * times] != 0
    next_ok = flags_ref[columns * times + 1] != 0
    for t in range(times):
        acc_ref[...] = jnp.zeros_like(acc_ref)
        max_ref[...] = jnp.full_like(max_ref, NEG)
        for c in range(columns):
            before, own, after = kv_refs[3 * c : 3 * c + 3]

            @pl.when(flags_ref[c * times + t] != 0)
            def _():
                window = []
                for w in range(t - 1, t + 2):
                    if w < 0:
                        window.append((before, 0, prev_ok))
                    elif w >= times:
                        window.append((after, 0, next_ok))
                    else:
                        window.append((own, w, None))
                query = q_ref[t]
                scores = []
                for ref, w, ok in window:
                    part = lax.dot_general(
                        query, ref[0, w], (((1,), (1,)), ((), ())), preferred_element_type=jnp.float32
                    )
                    scores.append(part if ok is None else jnp.where(ok, part, NEG))
                top = functools.reduce(jnp.maximum, scores)
                top = jnp.max(top, axis=1, keepdims=True)
                old = max_ref[...]
                new = jnp.maximum(old, top)
                max_ref[...] = new
                fade = jnp.exp2((old - new) * SCALE2)
                wide = jnp.concatenate([new] * (TILE // HD), axis=1)
                total = jnp.concatenate([fade, fade], axis=1) * acc_ref[...]
                for (ref, w, _), part in zip(window, scores):
                    weights = jnp.exp2((part - wide) * SCALE2).astype(jnp.bfloat16)
                    values = jnp.concatenate([ref[1, w], ones], axis=1)
                    total += jnp.dot(weights, values, preferred_element_type=jnp.float32)
                acc_ref[...] = total

        sums = acc_ref[:, HD:]
        some = sums > 0
        safe = jnp.where(some, sums, 1.0)
        o_ref[t] = (acc_ref[:, :HD] / safe).astype(o_ref.dtype)
        lse = jnp.where(some, max_ref[...] * SCALE2 + jnp.log2(safe), NEG)
        stat_ref[t] = jnp.where(lanes == head, lse, stat_ref[t])

    @pl.when(head == heads - 1)
    def _():
        for t in range(times):
            lse_ref[t] = jnp.transpose(stat_ref[t])[:STATS]


def partial_attention(flags, query, columns, dtype):
    times, _, features = query.shape
    heads = features // HD
    specs, operands = [], []
    for column in columns:
        for array in column:
            shape = (2, array.shape[1], TILE, HD)
            specs.append(pl.BlockSpec(shape, lambda h: (0, 0, 0, h)))
            operands.append(array)
    work = heads * times * len(columns) * 3 * TILE * TILE
    return pl.pallas_call(
        functools.partial(partial_kernel, times, len(columns), heads),
        grid=(heads,),
        out_shape=(
            jax.ShapeDtypeStruct((times, TILE, features), dtype),
            jax.ShapeDtypeStruct((times, STATS, TILE), jnp.float32),
        ),
        in_specs=[
            pl.BlockSpec(memory_space=pltpu.SMEM),
            pl.BlockSpec((times, TILE, HD), lambda h: (0, 0, h)),
            *specs,
        ],
        out_specs=(
            pl.BlockSpec((times, TILE, HD), lambda h: (0, 0, h)),
            pl.BlockSpec((times, STATS, TILE), lambda h: (0, 0, 0)),
        ),
        scratch_shapes=[
            pltpu.VMEM((TILE, 2 * HD), jnp.float32),
            pltpu.VMEM((TILE, HD), jnp.float32),
            pltpu.VMEM((times, TILE, HD), jnp.float32),
        ],
        compiler_params=pltpu.CompilerParams(vmem_limit_bytes=32 * 1024 * 1024),
        cost_estimate=pl.CostEstimate(
            flops=work * 8 * HD, bytes_accessed=2 * query.size * 8, transcendentals=work
        ),
    )(flags, query, *operands)


def combine_kernel(times, heads, parts, gate_ref, *refs):
    o_refs, lse_refs, out_ref = refs[:parts], refs[parts : 2 * parts], refs[2 * parts]
    pad = jnp.zeros((HD - STATS, TILE), jnp.float32)
    for t in range(times):
        lses = [ref[t] for ref in lse_refs]
        top = functools.reduce(jnp.maximum, lses)
        raised = [jnp.exp2(lse - top) for lse in lses]
        total = functools.reduce(jnp.add, raised)
        shares = [jnp.transpose(jnp.concatenate([one / total, pad], axis=0)) for one in raised]
        for h in range(heads):
            columns = slice(h * HD, (h + 1) * HD)
            result = functools.reduce(
                jnp.add,
                [
                    share[:, h : h + 1] * ref[t, :, columns].astype(jnp.float32)
                    for share, ref in zip(shares, o_refs)
                ],
            )
            out_ref[t, :, columns] = (result * gate_ref[t : t + 1, columns]).astype(out_ref.dtype)


def combine(gate, partials):
    first = partials[0][0]
    times, _, features = first.shape
    return pl.pallas_call(
        functools.partial(combine_kernel, times, features // HD, len(partials)),
        out_shape=jax.ShapeDtypeStruct(first.shape, jnp.bfloat16),
        compiler_params=pltpu.CompilerParams(vmem_limit_bytes=32 * 1024 * 1024),
        cost_estimate=pl.CostEstimate(
            flops=first.size * 8, bytes_accessed=first.size * 12, transcendentals=0
        ),
    )(gate, *[o for o, _ in partials], *[lse for _, lse in partials])


def gate_of(timesteps, gate_weight):
    half_freq = FREQ // 2
    frequencies = jnp.exp(-math.log(10000.0) * jnp.arange(half_freq, dtype=jnp.float32) / half_freq)
    angles = timesteps.astype(jnp.float32)[:, None] * frequencies[None, :]
    embedding = jnp.concatenate([jnp.cos(angles), jnp.sin(angles)], axis=1)
    return jnp.dot(
        embedding, gate_weight, precision=lax.Precision.HIGHEST, preferred_element_type=jnp.float32
    )


def with_edges(kv):
    size = lax.axis_size("tm")
    up = [(i, i + 1) for i in range(size - 1)]
    down = [(i + 1, i) for i in range(size - 1)]
    before = lax.ppermute(kv[:, -1:], "tm", up)
    after = lax.ppermute(kv[:, :1], "tm", down)
    return before, kv, after


def local_loop_of_four(query_field, key_field, value_field, tile_offsets, timesteps, gate_weight):
    times = query_field.shape[0] // TILE_T
    features = query_field.shape[3]
    tiled = (times, TILE, features)
    query, key, value = (x.reshape(tiled) for x in (query_field, key_field, value_field))
    me = lax.axis_index("lon")
    partner = me + 1 - 2 * (me % 2)
    across = 3 - me
    partners = [(0, 1), (1, 0), (2, 3), (3, 2)]
    visits = [(0, 3), (3, 0), (1, 2), (2, 1)]
    time_place = lax.axis_index("tm")
    ends = jnp.stack([time_place > 0, time_place < lax.axis_size("tm") - 1])
    offsets = tile_offsets[:, 0]
    across_offsets = lax.ppermute(offsets, "lon", visits)

    def used(column, home, shift):
        return (column - home - shift + 8) % 4 != 2

    def flags(*masks):
        return jnp.concatenate([*masks, ends]).astype(jnp.int32)

    always = jnp.ones((times,), jnp.bool_)
    flags_own = flags(always)
    flags_partner = flags(used(partner, me, offsets))
    flags_visit = flags(used(me, across, across_offsets), used(partner, across, across_offsets))
    gate_rows = gate_of(timesteps, gate_weight)
    width = CHUNK * HD
    pieces = []
    for start in range(0, features, width):
        part = slice(start, min(start + width, features))
        own = jnp.stack([key[:, :, part], value[:, :, part]])
        mine = query[:, :, part]
        other = lax.ppermute(own, "lon", partners)
        visitor = lax.ppermute(mine, "lon", visits)
        pieces.append((part, mine, visitor, with_edges(own), other))
    pieces = [(part, mine, visitor, own, with_edges(other)) for part, mine, visitor, own, other in pieces]
    results = []
    for part, mine, visitor, own, other in pieces:
        sent = partial_attention(flags_visit, visitor, [own, other], jnp.bfloat16)
        back = tuple(lax.ppermute(x, "lon", visits) for x in sent)
        first = partial_attention(flags_own, mine, [own], jnp.float32)
        second = partial_attention(flags_partner, mine, [other], jnp.float32)
        results.append(combine(gate_rows[:, part], [first, second, back]))
    return jnp.concatenate(results, axis=2).reshape(query_field.shape)


def from_behind(block, axis, distance):
    devices = range(lax.axis_size(axis))
    route = [((i - distance) % len(devices), i) for i in devices]
    return lax.ppermute(block, axis, route)


def extended_2(x, sides, width):
    for axis, dim in sides:
        size, length = (lax.axis_size(axis), x.shape[dim])
        up = [(i, (i + 1) % size) for i in range(size - 1)]
        down = [(j, i) for i, j in up]
        last = lax.slice_in_dim(x, length - width, length, axis=dim)
        leading = lax.slice_in_dim(x, 0, width, axis=dim)
        before = lax.ppermute(last, axis, up)
        after = lax.ppermute(leading, axis, down)
        x = jnp.concatenate([before, x, after], axis=dim)
    return x


def start_at(*entries):
    return tuple((jnp.asarray(entry).astype(jnp.int32) for entry in entries))


def lon_extend(column_block):
    pieces = {}
    for shift_by in (2, 1, -1, -2):
        pieces[shift_by] = from_behind(column_block, "lon", shift_by)
    return jnp.concatenate([pieces[2], pieces[1], column_block, pieces[-1], pieces[-2]], axis=4)


def local_any_loop(query_field, key_field, value_field, tile_offsets, timesteps, gate_weight):
    tiles_here = query_field.shape[0] // TILE_T
    features = query_field.shape[3]
    heads_here = features // HD
    tile_size = TILE_T * TILE_H * TILE_W
    tile_first = lax.axis_index("tm") * tiles_here
    time_count = tiles_here * lax.axis_size("tm")
    tiled_shape = (tiles_here, TILE_T, TILE_H, TILE_W, features)
    stacked = jnp.stack([key_field.reshape(tiled_shape), value_field.reshape(tiled_shape)], axis=1)
    rimmed = extended_2(stacked, (("tm", 0),), 1)
    extended = lon_extend(rimmed)
    half_freq = FREQ // 2
    frequencies = jnp.exp(-math.log(10000.0) * jnp.arange(half_freq, dtype=jnp.float32) / half_freq)
    angles = timesteps.astype(jnp.float32)[:, None] * frequencies[None, :]
    embedding = jnp.concatenate([jnp.cos(angles), jnp.sin(angles)], axis=1)
    gate_rows = jnp.dot(
        embedding, gate_weight, precision=lax.Precision.HIGHEST, preferred_element_type=jnp.float32
    )
    query_tiles = query_field.reshape(tiled_shape)
    inv_root = 1.0 / math.sqrt(HD)
    window_rows = 3 * TILE_T * TILE_H * 3 * TILE_W

    def one_pair(pair_index):
        tile_index = pair_index // heads_here
        head_index = pair_index % heads_here
        lon_shift = tile_offsets[tile_index, 0]
        window = lax.dynamic_slice(
            extended,
            start_at(tile_index, 0, 0, 0, (lon_shift + 1) * TILE_W, head_index * HD),
            (3, 2, TILE_T, TILE_H, 3 * TILE_W, HD),
        )
        key_rows = window[:, 0].reshape(window_rows, HD)
        value_rows = window[:, 1].reshape(window_rows, HD)
        query_rows = lax.dynamic_slice(
            query_tiles,
            start_at(tile_index, 0, 0, 0, head_index * HD),
            (1, TILE_T, TILE_H, TILE_W, HD),
        ).reshape(tile_size, HD)
        scores = (
            lax.dot_general(
                query_rows, key_rows, (((1,), (1,)), ((), ())), preferred_element_type=jnp.float32
            )
            * inv_root
        )
        window_times = tile_first + tile_index - 1 + jnp.arange(3, dtype=jnp.int32)
        usable = (window_times >= 0) & (window_times < time_count)
        scores = jnp.where(
            usable[None, :, None], scores.reshape(tile_size, 3, window_rows // 3), -1e30
        )
        scores = scores.reshape(tile_size, window_rows)
        row_max = jnp.max(scores, axis=1, keepdims=True)
        raised = jnp.exp(scores - row_max)
        totals = jnp.sum(raised, axis=1, keepdims=True)
        weights = raised.astype(jnp.bfloat16)
        weighted = jnp.dot(weights, value_rows, preferred_element_type=jnp.float32)
        gate_part = lax.dynamic_slice(gate_rows, start_at(tile_index, head_index * HD), (1, HD))
        return (weighted / totals * gate_part).astype(jnp.bfloat16)

    results = lax.map(one_pair, jnp.arange(tiles_here * heads_here, dtype=jnp.int32))
    results = results.reshape(tiles_here, heads_here, TILE_T, TILE_H, TILE_W, HD)
    results = jnp.transpose(results, (0, 2, 3, 4, 1, 5))
    return results.reshape(tiles_here * TILE_T, TILE_H, TILE_W, features)


def solution(mesh):
    local = local_loop_of_four if mesh.shape["lon"] == 4 else local_any_loop
    return jax.shard_map(
        local,
        mesh=mesh,
        in_specs=(
            P("tm", None, "lon", "head"),
            P("tm", None, "lon", "head"),
            P("tm", None, "lon", "head"),
            P("tm", "lon"),
            P("tm"),
            P(None, "head"),
        ),
        out_specs=P("tm", None, "lon", "head"),
        check_vma=False,
    )
```

```python
import functools
import math

import jax
import jax.numpy as jnp
from jax import lax
from jax.experimental import pallas as pl
from jax.experimental.pallas import tpu as pltpu
from jax.sharding import PartitionSpec as P

HD = 128
FREQ = 256
TILE_T = 6
TILE_H = 8
TILE_W = 8
TILE = TILE_T * TILE_H * TILE_W
SCALE2 = math.log2(math.e) / math.sqrt(HD)
BIG = 1e30
MESH = pl.DeviceIdType.MESH
OWN, VISIT = 0, 1
LON, QUERY, UP, DOWN, UP2, DOWN2, BACK, BACK_LSE = range(8)


def attention_kernel(
    times,
    heads,
    offset_ref,
    key_ref,
    value_ref,
    query_ref,
    gate_ref,
    out_ref,
    kv,
    queries,
    scores,
    o_send,
    o_back,
    lse_send,
    lse_back,
    o_own,
    lse_own,
    staged,
    cap_own,
    cap_send,
    cap_visit,
    load_sem,
    send_sem,
    recv_sem,
    cap_sem,
    out_sem,
):
    me = lax.axis_index("lon")
    partner = me + 1 - 2 * (me % 2)
    across = 3 - me
    place = lax.axis_index("tm")
    last = lax.axis_size("tm") - 1
    has_before, has_after = place > 0, place < last
    end = times + 1

    def lanes_of(h):
        return pl.ds(pl.multiple_of(h * HD, HD), HD)

    def loads(h):
        inner = pl.ds(1, times)
        return [
            pltpu.make_async_copy(source.at[:, :, lanes_of(h)], target, load_sem.at[i, h])
            for i, (source, target) in enumerate(
                [
                    (key_ref, kv.at[h, 0, 0, inner]),
                    (value_ref, kv.at[h, 0, 1, inner]),
                    (query_ref, queries.at[h, OWN]),
                ]
            )
        ]

    def remote(kind, h, source, target, device):
        return pltpu.make_async_remote_copy(
            src_ref=source,
            dst_ref=target,
            send_sem=send_sem.at[kind, h],
            recv_sem=recv_sem.at[kind, h],
            device_id=device,
            device_id_type=MESH,
        )

    def lon_copy(h):
        inner = pl.ds(1, times)
        return remote(LON, h, kv.at[h, 0, :, inner], kv.at[h, 1, :, inner], {"lon": partner})

    def query_copy(h):
        return remote(QUERY, h, queries.at[h, OWN], queries.at[h, VISIT], {"lon": across})

    def up_copy(h, c):
        return remote((UP, UP2)[c], h, kv.at[h, c, :, times], kv.at[h, c, :, 0], {"tm": place + 1})

    def down_copy(h, c):
        return remote((DOWN, DOWN2)[c], h, kv.at[h, c, :, 1], kv.at[h, c, :, end], {"tm": place - 1})

    def back_copy(h):
        return remote(BACK, h, o_send.at[h], o_back.at[h], {"lon": across})

    def back_lse_copy(h):
        return remote(BACK_LSE, h, lse_send.at[h], lse_back.at[h], {"lon": across})

    def out_copy(h):
        return pltpu.make_async_copy(staged.at[h], out_ref.at[:, :, lanes_of(h)], out_sem.at[h])

    cap_copy = pltpu.make_async_remote_copy(
        src_ref=cap_send,
        dst_ref=cap_visit,
        send_sem=cap_sem.at[0],
        recv_sem=cap_sem.at[1],
        device_id={"lon": across},
        device_id_type=MESH,
    )

    def load_all(h, carry):
        for copy in loads(h):
            copy.start()
        return carry

    lax.fori_loop(0, heads, load_all, 0)

    barrier = pltpu.get_barrier_semaphore()
    for neighbour in (partner, across):
        pl.semaphore_signal(barrier, inc=1, device_id={"lon": neighbour}, device_id_type=MESH)

    @pl.when(has_before)
    def _():
        pl.semaphore_signal(barrier, inc=1, device_id={"tm": place - 1}, device_id_type=MESH)

    @pl.when(has_after)
    def _():
        pl.semaphore_signal(barrier, inc=1, device_id={"tm": place + 1}, device_id_type=MESH)

    cap_own[...] = jnp.full_like(cap_own, BIG)
    cap_send[...] = jnp.full_like(cap_send, BIG)
    across_partner = across + 1 - 2 * (across % 2)
    for t in range(times):
        shift = offset_ref[t, 0]

        def cap(column):
            return jnp.where(lax.rem(column - me - shift + 8, 4) == 2, -BIG, BIG)

        cap_own[2 * t + 1 : 2 * t + 2] = jnp.full((1, HD), cap(partner), jnp.float32)
        cap_send[2 * t : 2 * t + 1] = jnp.full((1, HD), cap(across), jnp.float32)
        cap_send[2 * t + 1 : 2 * t + 2] = jnp.full((1, HD), cap(across_partner), jnp.float32)

    def blank(slot):
        def step(h, carry):
            for c in range(2):
                for i in range(2):
                    kv[h, c, i, slot] = jnp.zeros((TILE, HD), jnp.bfloat16)
            return carry

        lax.fori_loop(0, heads, step, 0)

    @pl.when(jnp.logical_not(has_before))
    def _():
        blank(0)

    @pl.when(jnp.logical_not(has_after))
    def _():
        blank(end)

    pl.semaphore_wait(barrier, 2 + has_before.astype(jnp.int32) + has_after.astype(jnp.int32))
    cap_copy.start()

    def send_first(h):
        for copy in loads(h):
            copy.wait()
        lon_copy(h).start()
        query_copy(h).start()

        @pl.when(has_after)
        def _():
            up_copy(h, 0).start()

        @pl.when(has_before)
        def _():
            down_copy(h, 0).start()

    def forward(h):
        lon_copy(h).wait_recv()

        @pl.when(has_after)
        def _():
            up_copy(h, 1).start()

        @pl.when(has_before)
        def _():
            down_copy(h, 1).start()

    send_first(0)
    send_first(1)
    cap_copy.wait()
    forward(0)

    before_cap = jnp.where(has_before, BIG, -BIG)
    after_cap = jnp.where(has_after, BIG, -BIG)
    ones = jnp.ones((TILE, HD), jnp.bfloat16)
    wins = [(c, w) for c in range(2) for w in range(3)]

    def score(h, whose, t, slot):
        scaled = queries[h, whose, t].astype(jnp.float32) * SCALE2
        high = scaled.astype(jnp.bfloat16)
        low = (scaled - high.astype(jnp.float32)).astype(jnp.bfloat16)
        query = jnp.concatenate([high, low], axis=1)
        for i, (c, w) in enumerate(wins):
            keys = kv[h, c, 0, t + w]
            keys = jnp.concatenate([keys, keys], axis=1)
            scores[slot, :, i * TILE : (i + 1) * TILE] = lax.dot_general(
                query, keys, (((1,), (1,)), ((), ())), preferred_element_type=jnp.float32
            )

    def attend(h, whose, t, slot):
        cap_ref = cap_visit if whose == VISIT else cap_own
        caps, tops = [], []
        for i, (c, w) in enumerate(wins):
            limit = cap_ref[2 * t + c : 2 * t + c + 1]
            if t + w == 0:
                limit = jnp.minimum(limit, before_cap)
            if t + w == end:
                limit = jnp.minimum(limit, after_cap)
            caps.append(limit)
            part = [
                scores[slot, :, i * TILE + j * HD : i * TILE + (j + 1) * HD] for j in range(TILE // HD)
            ]
            tops.append(jnp.minimum(functools.reduce(jnp.maximum, part), limit))
        top = jnp.max(functools.reduce(jnp.maximum, tops), axis=1, keepdims=True)
        total = None
        for i, (c, w) in enumerate(wins):
            base = jnp.maximum(top, -caps[i])
            base = jnp.concatenate([base] * (TILE // HD), axis=1)
            weights = jnp.exp2(scores[slot, :, i * TILE : (i + 1) * TILE] - base).astype(jnp.bfloat16)
            values = jnp.concatenate([kv[h, c, 1, t + w], ones], axis=1)
            part = jnp.dot(weights, values, preferred_element_type=jnp.float32)
            total = part if total is None else total + part
        sums = total[:, HD:]
        return total[:, :HD] / sums, top + jnp.log2(sums)

    def combine(h):
        back_copy(h).wait_recv()
        back_lse_copy(h).wait_recv()
        pad = jnp.zeros((HD - 8, TILE), jnp.float32)
        returned = jnp.transpose(jnp.concatenate([lse_back[h], pad], axis=0))
        slot = h % 2
        for t in range(times):
            mine = lse_own[slot, t]
            theirs = jnp.broadcast_to(returned[:, t : t + 1], mine.shape)
            top = jnp.maximum(mine, theirs)
            mine, theirs = jnp.exp2(mine - top), jnp.exp2(theirs - top)
            gate = gate_ref[t : t + 1, lanes_of(h)]
            mixed = o_own[slot, t] * mine + o_back[h, t].astype(jnp.float32) * theirs
            staged[h, t] = (mixed / (mine + theirs) * gate).astype(jnp.bfloat16)
        out_copy(h).start()

    first_lane = lax.broadcasted_iota(jnp.int32, (TILE, HD), 1) == 0

    def step(h, carry):
        @pl.when(h + 2 < heads)
        def _():
            send_first(h + 2)

        @pl.when(h + 1 < heads)
        def _():
            forward(h + 1)

        query_copy(h).wait_recv()

        @pl.when(has_before)
        def _():
            up_copy(h, 0).wait_recv()
            up_copy(h, 1).wait_recv()

        @pl.when(has_after)
        def _():
            down_copy(h, 0).wait_recv()
            down_copy(h, 1).wait_recv()

        slot = h % 2
        score(h, VISIT, 0, 0)
        score(h, VISIT, 1, 1)
        o0, lse0 = attend(h, VISIT, 0, 0)
        o_send[h, 0] = o0.astype(jnp.bfloat16)
        score(h, OWN, 0, 0)
        o1, lse1 = attend(h, VISIT, 1, 1)
        o_send[h, 1] = o1.astype(jnp.bfloat16)
        lse_send[h] = jnp.transpose(jnp.where(first_lane, lse0, lse1))[:8]
        back_copy(h).start()
        back_lse_copy(h).start()
        score(h, OWN, 1, 1)
        for t in range(times):
            o, lse = attend(h, OWN, t, t)
            o_own[slot, t] = o
            lse_own[slot, t] = lse

        @pl.when(h > 0)
        def _():
            combine(h - 1)

        return carry

    lax.fori_loop(0, heads, step, 0)
    combine(heads - 1)

    def finish(h, carry):
        out_copy(h).wait()
        for copy in (lon_copy(h), query_copy(h), back_copy(h), back_lse_copy(h)):
            copy.wait_send()

        @pl.when(has_after)
        def _():
            up_copy(h, 0).wait_send()
            up_copy(h, 1).wait_send()

        @pl.when(has_before)
        def _():
            down_copy(h, 0).wait_send()
            down_copy(h, 1).wait_send()

        return carry

    lax.fori_loop(0, heads, finish, 0)


def gate_of(timesteps, gate_weight):
    half_freq = FREQ // 2
    frequencies = jnp.exp(-math.log(10000.0) * jnp.arange(half_freq, dtype=jnp.float32) / half_freq)
    angles = timesteps.astype(jnp.float32)[:, None] * frequencies[None, :]
    embedding = jnp.concatenate([jnp.cos(angles), jnp.sin(angles)], axis=1)
    return jnp.dot(
        embedding, gate_weight, precision=lax.Precision.HIGHEST, preferred_element_type=jnp.float32
    )


def local_loop_of_four(query_field, key_field, value_field, tile_offsets, timesteps, gate_weight):
    times = query_field.shape[0] // TILE_T
    features = query_field.shape[3]
    heads = features // HD
    tiled = (times, TILE, features)
    query, key, value = (x.reshape(tiled) for x in (query_field, key_field, value_field))
    work = heads * times * 12 * TILE * TILE
    per_head = (heads, times, TILE, HD)
    result = pl.pallas_call(
        functools.partial(attention_kernel, times, heads),
        out_shape=jax.ShapeDtypeStruct(tiled, jnp.bfloat16),
        in_specs=[
            pl.BlockSpec(memory_space=pltpu.SMEM),
            pl.BlockSpec(memory_space=pl.ANY),
            pl.BlockSpec(memory_space=pl.ANY),
            pl.BlockSpec(memory_space=pl.ANY),
            pl.BlockSpec(memory_space=pltpu.VMEM),
        ],
        out_specs=pl.BlockSpec(memory_space=pl.ANY),
        scratch_shapes=[
            pltpu.VMEM((heads, 2, 2, times + 2, TILE, HD), jnp.bfloat16),
            pltpu.VMEM((heads, 2, times, TILE, HD), jnp.bfloat16),
            pltpu.VMEM((2, TILE, 6 * TILE), jnp.float32),
            pltpu.VMEM(per_head, jnp.bfloat16),
            pltpu.VMEM(per_head, jnp.bfloat16),
            pltpu.VMEM((heads, 8, TILE), jnp.float32),
            pltpu.VMEM((heads, 8, TILE), jnp.float32),
            pltpu.VMEM((2, times, TILE, HD), jnp.float32),
            pltpu.VMEM((2, times, TILE, HD), jnp.float32),
            pltpu.VMEM(per_head, jnp.bfloat16),
            pltpu.VMEM((8, HD), jnp.float32),
            pltpu.VMEM((8, HD), jnp.float32),
            pltpu.VMEM((8, HD), jnp.float32),
            pltpu.SemaphoreType.DMA((3, heads)),
            pltpu.SemaphoreType.DMA((8, heads)),
            pltpu.SemaphoreType.DMA((8, heads)),
            pltpu.SemaphoreType.DMA((2,)),
            pltpu.SemaphoreType.DMA((heads,)),
        ],
        compiler_params=pltpu.CompilerParams(
            collective_id=0, has_side_effects=True, vmem_limit_bytes=52 * 1024 * 1024
        ),
        cost_estimate=pl.CostEstimate(
            flops=work * 4 * HD, bytes_accessed=8 * query.size, transcendentals=work
        ),
    )(tile_offsets, key, value, query, gate_of(timesteps, gate_weight))
    return result.reshape(query_field.shape)


def from_behind(block, axis, distance):
    devices = range(lax.axis_size(axis))
    route = [((i - distance) % len(devices), i) for i in devices]
    return lax.ppermute(block, axis, route)


def extended_2(x, sides, width):
    for axis, dim in sides:
        size, length = (lax.axis_size(axis), x.shape[dim])
        up = [(i, (i + 1) % size) for i in range(size - 1)]
        down = [(j, i) for i, j in up]
        last = lax.slice_in_dim(x, length - width, length, axis=dim)
        leading = lax.slice_in_dim(x, 0, width, axis=dim)
        before = lax.ppermute(last, axis, up)
        after = lax.ppermute(leading, axis, down)
        x = jnp.concatenate([before, x, after], axis=dim)
    return x


def start_at(*entries):
    return tuple((jnp.asarray(entry).astype(jnp.int32) for entry in entries))


def lon_extend(column_block):
    pieces = {}
    for shift_by in (2, 1, -1, -2):
        pieces[shift_by] = from_behind(column_block, "lon", shift_by)
    return jnp.concatenate([pieces[2], pieces[1], column_block, pieces[-1], pieces[-2]], axis=4)


def local_any_loop(query_field, key_field, value_field, tile_offsets, timesteps, gate_weight):
    tiles_here = query_field.shape[0] // TILE_T
    features = query_field.shape[3]
    heads_here = features // HD
    tile_size = TILE_T * TILE_H * TILE_W
    tile_first = lax.axis_index("tm") * tiles_here
    time_count = tiles_here * lax.axis_size("tm")
    tiled_shape = (tiles_here, TILE_T, TILE_H, TILE_W, features)
    stacked = jnp.stack([key_field.reshape(tiled_shape), value_field.reshape(tiled_shape)], axis=1)
    rimmed = extended_2(stacked, (("tm", 0),), 1)
    extended = lon_extend(rimmed)
    half_freq = FREQ // 2
    frequencies = jnp.exp(-math.log(10000.0) * jnp.arange(half_freq, dtype=jnp.float32) / half_freq)
    angles = timesteps.astype(jnp.float32)[:, None] * frequencies[None, :]
    embedding = jnp.concatenate([jnp.cos(angles), jnp.sin(angles)], axis=1)
    gate_rows = jnp.dot(
        embedding, gate_weight, precision=lax.Precision.HIGHEST, preferred_element_type=jnp.float32
    )
    query_tiles = query_field.reshape(tiled_shape)
    inv_root = 1.0 / math.sqrt(HD)
    window_rows = 3 * TILE_T * TILE_H * 3 * TILE_W

    def one_pair(pair_index):
        tile_index = pair_index // heads_here
        head_index = pair_index % heads_here
        lon_shift = tile_offsets[tile_index, 0]
        window = lax.dynamic_slice(
            extended,
            start_at(tile_index, 0, 0, 0, (lon_shift + 1) * TILE_W, head_index * HD),
            (3, 2, TILE_T, TILE_H, 3 * TILE_W, HD),
        )
        key_rows = window[:, 0].reshape(window_rows, HD)
        value_rows = window[:, 1].reshape(window_rows, HD)
        query_rows = lax.dynamic_slice(
            query_tiles,
            start_at(tile_index, 0, 0, 0, head_index * HD),
            (1, TILE_T, TILE_H, TILE_W, HD),
        ).reshape(tile_size, HD)
        scores = (
            lax.dot_general(
                query_rows, key_rows, (((1,), (1,)), ((), ())), preferred_element_type=jnp.float32
            )
            * inv_root
        )
        window_times = tile_first + tile_index - 1 + jnp.arange(3, dtype=jnp.int32)
        usable = (window_times >= 0) & (window_times < time_count)
        scores = jnp.where(
            usable[None, :, None], scores.reshape(tile_size, 3, window_rows // 3), -1e30
        )
        scores = scores.reshape(tile_size, window_rows)
        row_max = jnp.max(scores, axis=1, keepdims=True)
        raised = jnp.exp(scores - row_max)
        totals = jnp.sum(raised, axis=1, keepdims=True)
        weights = raised.astype(jnp.bfloat16)
        weighted = jnp.dot(weights, value_rows, preferred_element_type=jnp.float32)
        gate_part = lax.dynamic_slice(gate_rows, start_at(tile_index, head_index * HD), (1, HD))
        return (weighted / totals * gate_part).astype(jnp.bfloat16)

    results = lax.map(one_pair, jnp.arange(tiles_here * heads_here, dtype=jnp.int32))
    results = results.reshape(tiles_here, heads_here, TILE_T, TILE_H, TILE_W, HD)
    results = jnp.transpose(results, (0, 2, 3, 4, 1, 5))
    return results.reshape(tiles_here * TILE_T, TILE_H, TILE_W, features)


def solution(mesh):
    local = local_loop_of_four if mesh.shape["lon"] == 4 else local_any_loop
    return jax.shard_map(
        local,
        mesh=mesh,
        in_specs=(
            P("tm", None, "lon", "head"),
            P("tm", None, "lon", "head"),
            P("tm", None, "lon", "head"),
            P("tm", "lon"),
            P("tm"),
            P(None, "head"),
        ),
        out_specs=P("tm", None, "lon", "head"),
        check_vma=False,
    )
```

```python
import functools
import math

import jax
import jax.numpy as jnp
from jax import lax
from jax.experimental import pallas as pl
from jax.experimental.pallas import tpu as pltpu
from jax.sharding import PartitionSpec as P

HD = 128
FREQ = 256
TILE_T = 6
TILE_H = 8
TILE_W = 8
TILE = TILE_T * TILE_H * TILE_W
SCALE2 = math.log2(math.e) / math.sqrt(HD)
BIG = 1e30
MESH = pl.DeviceIdType.MESH
OWN, VISIT = 0, 1
LON, QUERY, UP, DOWN, UP2, DOWN2, BACK_LSE, BACK = range(8)


def attention_kernel(
    times,
    heads,
    offset_ref,
    key_ref,
    value_ref,
    query_ref,
    gate_ref,
    out_ref,
    kv,
    queries,
    scores,
    o_send,
    o_back,
    lse_send,
    lse_back,
    o_own,
    lse_own,
    staged,
    cap_own,
    cap_send,
    cap_visit,
    load_sem,
    send_sem,
    recv_sem,
    cap_sem,
    out_sem,
):
    me = lax.axis_index("lon")
    partner = me + 1 - 2 * (me % 2)
    across = 3 - me
    place = lax.axis_index("tm")
    last = lax.axis_size("tm") - 1
    has_before, has_after = place > 0, place < last
    end = times + 1

    def lanes_of(h):
        return pl.ds(pl.multiple_of(h * HD, HD), HD)

    def loads(h, picked=(0, 1, 2)):
        inner = pl.ds(1, times)
        pairs = [
            (key_ref, kv.at[h, 0, 0, inner]),
            (value_ref, kv.at[h, 0, 1, inner]),
            (query_ref, queries.at[h, OWN]),
        ]
        return [
            pltpu.make_async_copy(pairs[i][0].at[:, :, lanes_of(h)], pairs[i][1], load_sem.at[i, h])
            for i in picked
        ]

    def remote(kind, h, source, target, device):
        return pltpu.make_async_remote_copy(
            src_ref=source,
            dst_ref=target,
            send_sem=send_sem.at[kind, h],
            recv_sem=recv_sem.at[kind, h],
            device_id=device,
            device_id_type=MESH,
        )

    def lon_copy(h):
        inner = pl.ds(1, times)
        return remote(LON, h, kv.at[h, 0, :, inner], kv.at[h, 1, :, inner], {"lon": partner})

    def query_copy(h):
        return remote(QUERY, h, queries.at[h, OWN], queries.at[h, VISIT], {"lon": across})

    def up_copy(h, c):
        return remote((UP, UP2)[c], h, kv.at[h, c, :, times], kv.at[h, c, :, 0], {"tm": place + 1})

    def down_copy(h, c):
        return remote((DOWN, DOWN2)[c], h, kv.at[h, c, :, 1], kv.at[h, c, :, end], {"tm": place - 1})

    def back_copy(h, t):
        return remote(BACK + t, h, o_send.at[h, t], o_back.at[h, t], {"lon": across})

    def back_lse_copy(h):
        return remote(BACK_LSE, h, lse_send.at[h], lse_back.at[h], {"lon": across})

    def out_copy(h):
        return pltpu.make_async_copy(staged.at[h], out_ref.at[:, :, lanes_of(h)], out_sem.at[h])

    cap_copy = pltpu.make_async_remote_copy(
        src_ref=cap_send,
        dst_ref=cap_visit,
        send_sem=cap_sem.at[0],
        recv_sem=cap_sem.at[1],
        device_id={"lon": across},
        device_id_type=MESH,
    )

    def load_all(h, carry):
        for copy in loads(h):
            copy.start()
        return carry

    lax.fori_loop(0, heads, load_all, 0)

    barrier = pltpu.get_barrier_semaphore()
    for neighbour in (partner, across):
        pl.semaphore_signal(barrier, inc=1, device_id={"lon": neighbour}, device_id_type=MESH)

    @pl.when(has_before)
    def _():
        pl.semaphore_signal(barrier, inc=1, device_id={"tm": place - 1}, device_id_type=MESH)

    @pl.when(has_after)
    def _():
        pl.semaphore_signal(barrier, inc=1, device_id={"tm": place + 1}, device_id_type=MESH)

    cap_own[...] = jnp.full_like(cap_own, BIG)
    cap_send[...] = jnp.full_like(cap_send, BIG)
    across_partner = across + 1 - 2 * (across % 2)
    for t in range(times):
        shift = offset_ref[t, 0]

        def cap(column):
            return jnp.where(lax.rem(column - me - shift + 8, 4) == 2, -BIG, BIG)

        cap_own[2 * t + 1 : 2 * t + 2] = jnp.full((1, HD), cap(partner), jnp.float32)
        cap_send[2 * t : 2 * t + 1] = jnp.full((1, HD), cap(across), jnp.float32)
        cap_send[2 * t + 1 : 2 * t + 2] = jnp.full((1, HD), cap(across_partner), jnp.float32)

    def blank(slot):
        def step(h, carry):
            for c in range(2):
                for i in range(2):
                    kv[h, c, i, slot] = jnp.zeros((TILE, HD), jnp.bfloat16)
            return carry

        lax.fori_loop(0, heads, step, 0)

    @pl.when(jnp.logical_not(has_before))
    def _():
        blank(0)

    @pl.when(jnp.logical_not(has_after))
    def _():
        blank(end)

    pl.semaphore_wait(barrier, 2 + has_before.astype(jnp.int32) + has_after.astype(jnp.int32))
    cap_copy.start()

    inner = (me == 1) | (me == 2)

    def send_queries(h, carry):
        query_copy(h).start()
        return carry

    def wait_queries(h, carry):
        loads(h, (2,))[0].wait()
        return carry

    def send_first(h):
        for copy in loads(h, (0, 1)):
            copy.wait()
        lon_copy(h).start()

        @pl.when(jnp.logical_not(inner))
        def _():
            query_copy(h).start()

        @pl.when(has_after)
        def _():
            up_copy(h, 0).start()

        @pl.when(has_before)
        def _():
            down_copy(h, 0).start()

    def forward(h):
        lon_copy(h).wait_recv()

        @pl.when(has_after)
        def _():
            up_copy(h, 1).start()

        @pl.when(has_before)
        def _():
            down_copy(h, 1).start()

    lax.fori_loop(0, heads, wait_queries, 0)
    send_first(0)

    @pl.when(inner)
    def _():
        lax.fori_loop(0, heads, send_queries, 0)

    send_first(1)
    cap_copy.wait()
    forward(0)

    before_cap = jnp.where(has_before, BIG, -BIG)
    after_cap = jnp.where(has_after, BIG, -BIG)
    ones = jnp.ones((TILE, HD), jnp.bfloat16)
    wins = [(c, w) for c in range(2) for w in range(3)]

    def score(h, whose, t, slot):
        scaled = queries[h, whose, t].astype(jnp.float32) * SCALE2
        high = scaled.astype(jnp.bfloat16)
        low = (scaled - high.astype(jnp.float32)).astype(jnp.bfloat16)
        query = jnp.concatenate([high, low], axis=1)
        for i, (c, w) in enumerate(wins):
            keys = kv[h, c, 0, t + w]
            keys = jnp.concatenate([keys, keys], axis=1)
            scores[slot, :, i * TILE : (i + 1) * TILE] = lax.dot_general(
                query, keys, (((1,), (1,)), ((), ())), preferred_element_type=jnp.float32
            )

    def attend(h, whose, t, slot):
        cap_ref = cap_visit if whose == VISIT else cap_own
        caps, tops = [], []
        for i, (c, w) in enumerate(wins):
            limit = cap_ref[2 * t + c : 2 * t + c + 1]
            if t + w == 0:
                limit = jnp.minimum(limit, before_cap)
            if t + w == end:
                limit = jnp.minimum(limit, after_cap)
            caps.append(limit)
            part = [
                scores[slot, :, i * TILE + j * HD : i * TILE + (j + 1) * HD] for j in range(TILE // HD)
            ]
            tops.append(jnp.minimum(functools.reduce(jnp.maximum, part), limit))
        top = jnp.max(functools.reduce(jnp.maximum, tops), axis=1, keepdims=True)
        total = None
        for i, (c, w) in enumerate(wins):
            base = jnp.maximum(top, -caps[i])
            base = jnp.concatenate([base] * (TILE // HD), axis=1)
            weights = jnp.exp2(scores[slot, :, i * TILE : (i + 1) * TILE] - base).astype(jnp.bfloat16)
            values = jnp.concatenate([kv[h, c, 1, t + w], ones], axis=1)
            part = jnp.dot(weights, values, preferred_element_type=jnp.float32)
            total = part if total is None else total + part
        sums = total[:, HD:]
        return total[:, :HD] / sums, top + jnp.log2(sums)

    def combine(h):
        for t in range(times):
            back_copy(h, t).wait_recv()
        back_lse_copy(h).wait_recv()
        pad = jnp.zeros((HD - times, TILE), jnp.float32)
        returned = jnp.transpose(jnp.concatenate([lse_back[h], pad], axis=0))
        slot = h % 2
        for t in range(times):
            mine = lse_own[slot, t]
            theirs = jnp.broadcast_to(returned[:, t : t + 1], mine.shape)
            top = jnp.maximum(mine, theirs)
            mine, theirs = jnp.exp2(mine - top), jnp.exp2(theirs - top)
            gate = gate_ref[t : t + 1, lanes_of(h)]
            mixed = o_own[slot, t] * mine + o_back[h, t].astype(jnp.float32) * theirs
            staged[h, t] = (mixed / (mine + theirs) * gate).astype(jnp.bfloat16)
        out_copy(h).start()

    first_lane = lax.broadcasted_iota(jnp.int32, (TILE, HD), 1) == 0

    def step(h, carry):
        @pl.when(h + 2 < heads)
        def _():
            send_first(h + 2)

        query_copy(h).wait_recv()

        @pl.when(has_before)
        def _():
            up_copy(h, 0).wait_recv()
            up_copy(h, 1).wait_recv()

        @pl.when(has_after)
        def _():
            down_copy(h, 0).wait_recv()
            down_copy(h, 1).wait_recv()

        slot = h % 2
        score(h, VISIT, 0, 0)
        score(h, VISIT, 1, 1)
        o0, lse0 = attend(h, VISIT, 0, 0)
        o_send[h, 0] = o0.astype(jnp.bfloat16)
        back_copy(h, 0).start()
        score(h, OWN, 0, 0)
        o1, lse1 = attend(h, VISIT, 1, 1)
        o_send[h, 1] = o1.astype(jnp.bfloat16)
        lse_send[h] = jnp.transpose(jnp.where(first_lane, lse0, lse1))[:times]
        back_copy(h, 1).start()
        back_lse_copy(h).start()

        @pl.when(h + 1 < heads)
        def _():
            forward(h + 1)

        score(h, OWN, 1, 1)
        for t in range(times):
            o, lse = attend(h, OWN, t, t)
            o_own[slot, t] = o
            lse_own[slot, t] = lse

        @pl.when(h > 0)
        def _():
            combine(h - 1)

        return carry

    lax.fori_loop(0, heads, step, 0)
    combine(heads - 1)

    def finish(h, carry):
        out_copy(h).wait()
        backs = [back_copy(h, t) for t in range(times)]
        for copy in (lon_copy(h), query_copy(h), back_lse_copy(h), *backs):
            copy.wait_send()

        @pl.when(has_after)
        def _():
            up_copy(h, 0).wait_send()
            up_copy(h, 1).wait_send()

        @pl.when(has_before)
        def _():
            down_copy(h, 0).wait_send()
            down_copy(h, 1).wait_send()

        return carry

    lax.fori_loop(0, heads, finish, 0)


def gate_of(timesteps, gate_weight):
    half_freq = FREQ // 2
    frequencies = jnp.exp(-math.log(10000.0) * jnp.arange(half_freq, dtype=jnp.float32) / half_freq)
    angles = timesteps.astype(jnp.float32)[:, None] * frequencies[None, :]
    embedding = jnp.concatenate([jnp.cos(angles), jnp.sin(angles)], axis=1)
    return jnp.dot(
        embedding, gate_weight, precision=lax.Precision.HIGHEST, preferred_element_type=jnp.float32
    )


def local_loop_of_four(query_field, key_field, value_field, tile_offsets, timesteps, gate_weight):
    times = query_field.shape[0] // TILE_T
    features = query_field.shape[3]
    heads = features // HD
    tiled = (times, TILE, features)
    query, key, value = (x.reshape(tiled) for x in (query_field, key_field, value_field))
    work = heads * times * 12 * TILE * TILE
    per_head = (heads, times, TILE, HD)
    result = pl.pallas_call(
        functools.partial(attention_kernel, times, heads),
        out_shape=jax.ShapeDtypeStruct(tiled, jnp.bfloat16),
        in_specs=[
            pl.BlockSpec(memory_space=pltpu.SMEM),
            pl.BlockSpec(memory_space=pl.ANY),
            pl.BlockSpec(memory_space=pl.ANY),
            pl.BlockSpec(memory_space=pl.ANY),
            pl.BlockSpec(memory_space=pltpu.VMEM),
        ],
        out_specs=pl.BlockSpec(memory_space=pl.ANY),
        scratch_shapes=[
            pltpu.VMEM((heads, 2, 2, times + 2, TILE, HD), jnp.bfloat16),
            pltpu.VMEM((heads, 2, times, TILE, HD), jnp.bfloat16),
            pltpu.VMEM((2, TILE, 6 * TILE), jnp.float32),
            pltpu.VMEM(per_head, jnp.bfloat16),
            pltpu.VMEM(per_head, jnp.bfloat16),
            pltpu.VMEM((heads, times, TILE), jnp.float32),
            pltpu.VMEM((heads, times, TILE), jnp.float32),
            pltpu.VMEM((2, times, TILE, HD), jnp.float32),
            pltpu.VMEM((2, times, TILE, HD), jnp.float32),
            pltpu.VMEM(per_head, jnp.bfloat16),
            pltpu.VMEM((8, HD), jnp.float32),
            pltpu.VMEM((8, HD), jnp.float32),
            pltpu.VMEM((8, HD), jnp.float32),
            pltpu.SemaphoreType.DMA((3, heads)),
            pltpu.SemaphoreType.DMA((7 + times, heads)),
            pltpu.SemaphoreType.DMA((7 + times, heads)),
            pltpu.SemaphoreType.DMA((2,)),
            pltpu.SemaphoreType.DMA((heads,)),
        ],
        compiler_params=pltpu.CompilerParams(
            collective_id=0, has_side_effects=True, vmem_limit_bytes=52 * 1024 * 1024
        ),
        cost_estimate=pl.CostEstimate(
            flops=work * 4 * HD, bytes_accessed=8 * query.size, transcendentals=work
        ),
    )(tile_offsets, key, value, query, gate_of(timesteps, gate_weight))
    return result.reshape(query_field.shape)


def from_behind(block, axis, distance):
    devices = range(lax.axis_size(axis))
    route = [((i - distance) % len(devices), i) for i in devices]
    return lax.ppermute(block, axis, route)


def extended_2(x, sides, width):
    for axis, dim in sides:
        size, length = (lax.axis_size(axis), x.shape[dim])
        up = [(i, (i + 1) % size) for i in range(size - 1)]
        down = [(j, i) for i, j in up]
        last = lax.slice_in_dim(x, length - width, length, axis=dim)
        leading = lax.slice_in_dim(x, 0, width, axis=dim)
        before = lax.ppermute(last, axis, up)
        after = lax.ppermute(leading, axis, down)
        x = jnp.concatenate([before, x, after], axis=dim)
    return x


def start_at(*entries):
    return tuple((jnp.asarray(entry).astype(jnp.int32) for entry in entries))


def lon_extend(column_block):
    pieces = {}
    for shift_by in (2, 1, -1, -2):
        pieces[shift_by] = from_behind(column_block, "lon", shift_by)
    return jnp.concatenate([pieces[2], pieces[1], column_block, pieces[-1], pieces[-2]], axis=4)


def local_any_loop(query_field, key_field, value_field, tile_offsets, timesteps, gate_weight):
    tiles_here = query_field.shape[0] // TILE_T
    features = query_field.shape[3]
    heads_here = features // HD
    tile_size = TILE_T * TILE_H * TILE_W
    tile_first = lax.axis_index("tm") * tiles_here
    time_count = tiles_here * lax.axis_size("tm")
    tiled_shape = (tiles_here, TILE_T, TILE_H, TILE_W, features)
    stacked = jnp.stack([key_field.reshape(tiled_shape), value_field.reshape(tiled_shape)], axis=1)
    rimmed = extended_2(stacked, (("tm", 0),), 1)
    extended = lon_extend(rimmed)
    half_freq = FREQ // 2
    frequencies = jnp.exp(-math.log(10000.0) * jnp.arange(half_freq, dtype=jnp.float32) / half_freq)
    angles = timesteps.astype(jnp.float32)[:, None] * frequencies[None, :]
    embedding = jnp.concatenate([jnp.cos(angles), jnp.sin(angles)], axis=1)
    gate_rows = jnp.dot(
        embedding, gate_weight, precision=lax.Precision.HIGHEST, preferred_element_type=jnp.float32
    )
    query_tiles = query_field.reshape(tiled_shape)
    inv_root = 1.0 / math.sqrt(HD)
    window_rows = 3 * TILE_T * TILE_H * 3 * TILE_W

    def one_pair(pair_index):
        tile_index = pair_index // heads_here
        head_index = pair_index % heads_here
        lon_shift = tile_offsets[tile_index, 0]
        window = lax.dynamic_slice(
            extended,
            start_at(tile_index, 0, 0, 0, (lon_shift + 1) * TILE_W, head_index * HD),
            (3, 2, TILE_T, TILE_H, 3 * TILE_W, HD),
        )
        key_rows = window[:, 0].reshape(window_rows, HD)
        value_rows = window[:, 1].reshape(window_rows, HD)
        query_rows = lax.dynamic_slice(
            query_tiles,
            start_at(tile_index, 0, 0, 0, head_index * HD),
            (1, TILE_T, TILE_H, TILE_W, HD),
        ).reshape(tile_size, HD)
        scores = (
            lax.dot_general(
                query_rows, key_rows, (((1,), (1,)), ((), ())), preferred_element_type=jnp.float32
            )
            * inv_root
        )
        window_times = tile_first + tile_index - 1 + jnp.arange(3, dtype=jnp.int32)
        usable = (window_times >= 0) & (window_times < time_count)
        scores = jnp.where(
            usable[None, :, None], scores.reshape(tile_size, 3, window_rows // 3), -1e30
        )
        scores = scores.reshape(tile_size, window_rows)
        row_max = jnp.max(scores, axis=1, keepdims=True)
        raised = jnp.exp(scores - row_max)
        totals = jnp.sum(raised, axis=1, keepdims=True)
        weights = raised.astype(jnp.bfloat16)
        weighted = jnp.dot(weights, value_rows, preferred_element_type=jnp.float32)
        gate_part = lax.dynamic_slice(gate_rows, start_at(tile_index, head_index * HD), (1, HD))
        return (weighted / totals * gate_part).astype(jnp.bfloat16)

    results = lax.map(one_pair, jnp.arange(tiles_here * heads_here, dtype=jnp.int32))
    results = results.reshape(tiles_here, heads_here, TILE_T, TILE_H, TILE_W, HD)
    results = jnp.transpose(results, (0, 2, 3, 4, 1, 5))
    return results.reshape(tiles_here * TILE_T, TILE_H, TILE_W, features)


def solution(mesh):
    local = local_loop_of_four if mesh.shape["lon"] == 4 else local_any_loop
    return jax.shard_map(
        local,
        mesh=mesh,
        in_specs=(
            P("tm", None, "lon", "head"),
            P("tm", None, "lon", "head"),
            P("tm", None, "lon", "head"),
            P("tm", "lon"),
            P("tm"),
            P(None, "head"),
        ),
        out_specs=P("tm", None, "lon", "head"),
        check_vma=False,
    )
```

```python
import functools
import math

import jax
import jax.numpy as jnp
from jax import lax
from jax.experimental import pallas as pl
from jax.experimental.pallas import tpu as pltpu
from jax.sharding import PartitionSpec as P

HD = 128
FREQ = 256
TILE_T = 6
TILE_H = 8
TILE_W = 8
TILE = TILE_T * TILE_H * TILE_W
SCALE2 = math.log2(math.e) / math.sqrt(HD)
BIG = 1e30
AHEAD = 4
MESH = pl.DeviceIdType.MESH
OWN, VISIT = 0, 1
LON, QUERY, UP, DOWN, UP2, DOWN2, BACK_LSE, BACK = range(8)


def attention_kernel(
    times,
    heads,
    offset_ref,
    key_ref,
    value_ref,
    query_ref,
    gate_ref,
    out_ref,
    kv,
    queries,
    scores,
    o_send,
    o_back,
    lse_send,
    lse_back,
    o_own,
    lse_own,
    staged,
    cap_own,
    cap_send,
    cap_visit,
    load_sem,
    send_sem,
    recv_sem,
    cap_sem,
    out_sem,
):
    me = lax.axis_index("lon")
    partner = me + 1 - 2 * (me % 2)
    across = 3 - me
    place = lax.axis_index("tm")
    last = lax.axis_size("tm") - 1
    has_before, has_after = place > 0, place < last
    end = times + 1

    def lanes_of(h):
        return pl.ds(pl.multiple_of(h * HD, HD), HD)

    def loads(h, picked=(0, 1, 2)):
        inner = pl.ds(1, times)
        pairs = [
            (key_ref, kv.at[h, 0, 0, inner]),
            (value_ref, kv.at[h, 0, 1, inner]),
            (query_ref, queries.at[h, OWN]),
        ]
        return [
            pltpu.make_async_copy(pairs[i][0].at[:, :, lanes_of(h)], pairs[i][1], load_sem.at[i, h])
            for i in picked
        ]

    def remote(kind, h, source, target, device):
        return pltpu.make_async_remote_copy(
            src_ref=source,
            dst_ref=target,
            send_sem=send_sem.at[kind, h],
            recv_sem=recv_sem.at[kind, h],
            device_id=device,
            device_id_type=MESH,
        )

    def lon_copy(h):
        inner = pl.ds(1, times)
        return remote(LON, h, kv.at[h, 0, :, inner], kv.at[h, 1, :, inner], {"lon": partner})

    def query_copy(h):
        return remote(QUERY, h, queries.at[h, OWN], queries.at[h, VISIT], {"lon": across})

    def up_copy(h, c):
        return remote((UP, UP2)[c], h, kv.at[h, c, :, times], kv.at[h, c, :, 0], {"tm": place + 1})

    def down_copy(h, c):
        return remote((DOWN, DOWN2)[c], h, kv.at[h, c, :, 1], kv.at[h, c, :, end], {"tm": place - 1})

    def back_copy(h, t):
        return remote(BACK + t, h, o_send.at[h, t], o_back.at[h, t], {"lon": across})

    def back_lse_copy(h):
        return remote(BACK_LSE, h, lse_send.at[h], lse_back.at[h], {"lon": across})

    def out_copy(h):
        return pltpu.make_async_copy(staged.at[h], out_ref.at[:, :, lanes_of(h)], out_sem.at[h])

    cap_copy = pltpu.make_async_remote_copy(
        src_ref=cap_send,
        dst_ref=cap_visit,
        send_sem=cap_sem.at[0],
        recv_sem=cap_sem.at[1],
        device_id={"lon": across},
        device_id_type=MESH,
    )

    def load_all(h, carry):
        for copy in loads(h):
            copy.start()
        return carry

    lax.fori_loop(0, heads, load_all, 0)

    barrier = pltpu.get_barrier_semaphore()
    for neighbour in (partner, across):
        pl.semaphore_signal(barrier, inc=1, device_id={"lon": neighbour}, device_id_type=MESH)

    @pl.when(has_before)
    def _():
        pl.semaphore_signal(barrier, inc=1, device_id={"tm": place - 1}, device_id_type=MESH)

    @pl.when(has_after)
    def _():
        pl.semaphore_signal(barrier, inc=1, device_id={"tm": place + 1}, device_id_type=MESH)

    cap_own[...] = jnp.full_like(cap_own, BIG)
    cap_send[...] = jnp.full_like(cap_send, BIG)
    across_partner = across + 1 - 2 * (across % 2)
    for t in range(times):
        shift = offset_ref[t, 0]

        def cap(column):
            return jnp.where(lax.rem(column - me - shift + 8, 4) == 2, -BIG, BIG)

        cap_own[2 * t + 1 : 2 * t + 2] = jnp.full((1, HD), cap(partner), jnp.float32)
        cap_send[2 * t : 2 * t + 1] = jnp.full((1, HD), cap(across), jnp.float32)
        cap_send[2 * t + 1 : 2 * t + 2] = jnp.full((1, HD), cap(across_partner), jnp.float32)

    def blank(slot):
        def step(h, carry):
            for c in range(2):
                for i in range(2):
                    kv[h, c, i, slot] = jnp.zeros((TILE, HD), jnp.bfloat16)
            return carry

        lax.fori_loop(0, heads, step, 0)

    @pl.when(jnp.logical_not(has_before))
    def _():
        blank(0)

    @pl.when(jnp.logical_not(has_after))
    def _():
        blank(end)

    pl.semaphore_wait(barrier, 2 + has_before.astype(jnp.int32) + has_after.astype(jnp.int32))
    cap_copy.start()

    inner = (me == 1) | (me == 2)

    def send_queries(h, carry):
        query_copy(h).start()
        return carry

    def wait_queries(h, carry):
        loads(h, (2,))[0].wait()
        return carry

    def send_first(h):
        for copy in loads(h, (0, 1)):
            copy.wait()
        lon_copy(h).start()

        @pl.when(jnp.logical_not(inner))
        def _():
            query_copy(h).start()

        @pl.when(has_after)
        def _():
            up_copy(h, 0).start()

        @pl.when(has_before)
        def _():
            down_copy(h, 0).start()

    def forward(h):
        lon_copy(h).wait_recv()

        @pl.when(has_after)
        def _():
            up_copy(h, 1).start()

        @pl.when(has_before)
        def _():
            down_copy(h, 1).start()

    lax.fori_loop(0, heads, wait_queries, 0)
    send_first(0)

    @pl.when(inner)
    def _():
        lax.fori_loop(0, heads, send_queries, 0)

    for h in range(1, min(AHEAD, heads)):
        send_first(h)
    cap_copy.wait()
    forward(0)

    before_cap = jnp.where(has_before, BIG, -BIG)
    after_cap = jnp.where(has_after, BIG, -BIG)
    ones = jnp.ones((TILE, HD), jnp.bfloat16)
    wins = [(c, w) for c in range(2) for w in range(3)]

    def score(h, whose, t, slot):
        scaled = queries[h, whose, t].astype(jnp.float32) * SCALE2
        high = scaled.astype(jnp.bfloat16)
        low = (scaled - high.astype(jnp.float32)).astype(jnp.bfloat16)
        query = jnp.concatenate([high, low], axis=1)
        for i, (c, w) in enumerate(wins):
            keys = kv[h, c, 0, t + w]
            keys = jnp.concatenate([keys, keys], axis=1)
            scores[slot, :, i * TILE : (i + 1) * TILE] = lax.dot_general(
                query, keys, (((1,), (1,)), ((), ())), preferred_element_type=jnp.float32
            )

    def attend(h, whose, t, slot):
        cap_ref = cap_visit if whose == VISIT else cap_own
        caps, tops = [], []
        for i, (c, w) in enumerate(wins):
            limit = cap_ref[2 * t + c : 2 * t + c + 1]
            if t + w == 0:
                limit = jnp.minimum(limit, before_cap)
            if t + w == end:
                limit = jnp.minimum(limit, after_cap)
            caps.append(limit)
            part = [
                scores[slot, :, i * TILE + j * HD : i * TILE + (j + 1) * HD] for j in range(TILE // HD)
            ]
            tops.append(jnp.minimum(functools.reduce(jnp.maximum, part), limit))
        top = jnp.max(functools.reduce(jnp.maximum, tops), axis=1, keepdims=True)
        total = None
        for i, (c, w) in enumerate(wins):
            base = jnp.maximum(top, -caps[i])
            base = jnp.concatenate([base] * (TILE // HD), axis=1)
            weights = jnp.exp2(scores[slot, :, i * TILE : (i + 1) * TILE] - base).astype(jnp.bfloat16)
            values = jnp.concatenate([kv[h, c, 1, t + w], ones], axis=1)
            part = jnp.dot(weights, values, preferred_element_type=jnp.float32)
            total = part if total is None else total + part
        sums = total[:, HD:]
        return total[:, :HD] / sums, top + jnp.log2(sums)

    def combine(h):
        for t in range(times):
            back_copy(h, t).wait_recv()
        back_lse_copy(h).wait_recv()
        pad = jnp.zeros((HD - times, TILE), jnp.float32)
        returned = jnp.transpose(jnp.concatenate([lse_back[h], pad], axis=0))
        slot = h % 2
        for t in range(times):
            mine = lse_own[slot, t]
            theirs = jnp.broadcast_to(returned[:, t : t + 1], mine.shape)
            top = jnp.maximum(mine, theirs)
            mine, theirs = jnp.exp2(mine - top), jnp.exp2(theirs - top)
            gate = gate_ref[t : t + 1, lanes_of(h)]
            mixed = o_own[slot, t] * mine + o_back[h, t].astype(jnp.float32) * theirs
            staged[h, t] = (mixed / (mine + theirs) * gate).astype(jnp.bfloat16)
        out_copy(h).start()

    first_lane = lax.broadcasted_iota(jnp.int32, (TILE, HD), 1) == 0

    def step(h, carry):
        @pl.when(h + AHEAD < heads)
        def _():
            send_first(h + AHEAD)

        query_copy(h).wait_recv()

        @pl.when(has_before)
        def _():
            up_copy(h, 0).wait_recv()
            up_copy(h, 1).wait_recv()

        @pl.when(has_after)
        def _():
            down_copy(h, 0).wait_recv()
            down_copy(h, 1).wait_recv()

        slot = h % 2
        score(h, VISIT, 0, 0)
        score(h, VISIT, 1, 1)
        o0, lse0 = attend(h, VISIT, 0, 0)
        o_send[h, 0] = o0.astype(jnp.bfloat16)
        back_copy(h, 0).start()
        score(h, OWN, 0, 0)
        o1, lse1 = attend(h, VISIT, 1, 1)
        o_send[h, 1] = o1.astype(jnp.bfloat16)
        lse_send[h] = jnp.transpose(jnp.where(first_lane, lse0, lse1))[:times]
        back_copy(h, 1).start()
        back_lse_copy(h).start()

        @pl.when(h + 1 < heads)
        def _():
            forward(h + 1)

        score(h, OWN, 1, 1)
        for t in range(times):
            o, lse = attend(h, OWN, t, t)
            o_own[slot, t] = o
            lse_own[slot, t] = lse

        @pl.when(h > 0)
        def _():
            combine(h - 1)

        return carry

    lax.fori_loop(0, heads, step, 0)
    combine(heads - 1)

    def finish(h, carry):
        out_copy(h).wait()
        backs = [back_copy(h, t) for t in range(times)]
        for copy in (lon_copy(h), query_copy(h), back_lse_copy(h), *backs):
            copy.wait_send()

        @pl.when(has_after)
        def _():
            up_copy(h, 0).wait_send()
            up_copy(h, 1).wait_send()

        @pl.when(has_before)
        def _():
            down_copy(h, 0).wait_send()
            down_copy(h, 1).wait_send()

        return carry

    lax.fori_loop(0, heads, finish, 0)


def gate_of(timesteps, gate_weight):
    half_freq = FREQ // 2
    frequencies = jnp.exp(-math.log(10000.0) * jnp.arange(half_freq, dtype=jnp.float32) / half_freq)
    angles = timesteps.astype(jnp.float32)[:, None] * frequencies[None, :]
    embedding = jnp.concatenate([jnp.cos(angles), jnp.sin(angles)], axis=1)
    return jnp.dot(
        embedding, gate_weight, precision=lax.Precision.HIGHEST, preferred_element_type=jnp.float32
    )


def local_loop_of_four(query_field, key_field, value_field, tile_offsets, timesteps, gate_weight):
    times = query_field.shape[0] // TILE_T
    features = query_field.shape[3]
    heads = features // HD
    tiled = (times, TILE, features)
    query, key, value = (x.reshape(tiled) for x in (query_field, key_field, value_field))
    work = heads * times * 12 * TILE * TILE
    per_head = (heads, times, TILE, HD)
    result = pl.pallas_call(
        functools.partial(attention_kernel, times, heads),
        out_shape=jax.ShapeDtypeStruct(tiled, jnp.bfloat16),
        in_specs=[
            pl.BlockSpec(memory_space=pltpu.SMEM),
            pl.BlockSpec(memory_space=pl.ANY),
            pl.BlockSpec(memory_space=pl.ANY),
            pl.BlockSpec(memory_space=pl.ANY),
            pl.BlockSpec(memory_space=pltpu.VMEM),
        ],
        out_specs=pl.BlockSpec(memory_space=pl.ANY),
        scratch_shapes=[
            pltpu.VMEM((heads, 2, 2, times + 2, TILE, HD), jnp.bfloat16),
            pltpu.VMEM((heads, 2, times, TILE, HD), jnp.bfloat16),
            pltpu.VMEM((2, TILE, 6 * TILE), jnp.float32),
            pltpu.VMEM(per_head, jnp.bfloat16),
            pltpu.VMEM(per_head, jnp.bfloat16),
            pltpu.VMEM((heads, times, TILE), jnp.float32),
            pltpu.VMEM((heads, times, TILE), jnp.float32),
            pltpu.VMEM((2, times, TILE, HD), jnp.float32),
            pltpu.VMEM((2, times, TILE, HD), jnp.float32),
            pltpu.VMEM(per_head, jnp.bfloat16),
            pltpu.VMEM((8, HD), jnp.float32),
            pltpu.VMEM((8, HD), jnp.float32),
            pltpu.VMEM((8, HD), jnp.float32),
            pltpu.SemaphoreType.DMA((3, heads)),
            pltpu.SemaphoreType.DMA((7 + times, heads)),
            pltpu.SemaphoreType.DMA((7 + times, heads)),
            pltpu.SemaphoreType.DMA((2,)),
            pltpu.SemaphoreType.DMA((heads,)),
        ],
        compiler_params=pltpu.CompilerParams(
            collective_id=0, has_side_effects=True, vmem_limit_bytes=52 * 1024 * 1024
        ),
        cost_estimate=pl.CostEstimate(
            flops=work * 4 * HD, bytes_accessed=8 * query.size, transcendentals=work
        ),
    )(tile_offsets, key, value, query, gate_of(timesteps, gate_weight))
    return result.reshape(query_field.shape)


def from_behind(block, axis, distance):
    devices = range(lax.axis_size(axis))
    route = [((i - distance) % len(devices), i) for i in devices]
    return lax.ppermute(block, axis, route)


def extended_2(x, sides, width):
    for axis, dim in sides:
        size, length = (lax.axis_size(axis), x.shape[dim])
        up = [(i, (i + 1) % size) for i in range(size - 1)]
        down = [(j, i) for i, j in up]
        last = lax.slice_in_dim(x, length - width, length, axis=dim)
        leading = lax.slice_in_dim(x, 0, width, axis=dim)
        before = lax.ppermute(last, axis, up)
        after = lax.ppermute(leading, axis, down)
        x = jnp.concatenate([before, x, after], axis=dim)
    return x


def start_at(*entries):
    return tuple((jnp.asarray(entry).astype(jnp.int32) for entry in entries))


def lon_extend(column_block):
    pieces = {}
    for shift_by in (2, 1, -1, -2):
        pieces[shift_by] = from_behind(column_block, "lon", shift_by)
    return jnp.concatenate([pieces[2], pieces[1], column_block, pieces[-1], pieces[-2]], axis=4)


def local_any_loop(query_field, key_field, value_field, tile_offsets, timesteps, gate_weight):
    tiles_here = query_field.shape[0] // TILE_T
    features = query_field.shape[3]
    heads_here = features // HD
    tile_size = TILE_T * TILE_H * TILE_W
    tile_first = lax.axis_index("tm") * tiles_here
    time_count = tiles_here * lax.axis_size("tm")
    tiled_shape = (tiles_here, TILE_T, TILE_H, TILE_W, features)
    stacked = jnp.stack([key_field.reshape(tiled_shape), value_field.reshape(tiled_shape)], axis=1)
    rimmed = extended_2(stacked, (("tm", 0),), 1)
    extended = lon_extend(rimmed)
    half_freq = FREQ // 2
    frequencies = jnp.exp(-math.log(10000.0) * jnp.arange(half_freq, dtype=jnp.float32) / half_freq)
    angles = timesteps.astype(jnp.float32)[:, None] * frequencies[None, :]
    embedding = jnp.concatenate([jnp.cos(angles), jnp.sin(angles)], axis=1)
    gate_rows = jnp.dot(
        embedding, gate_weight, precision=lax.Precision.HIGHEST, preferred_element_type=jnp.float32
    )
    query_tiles = query_field.reshape(tiled_shape)
    inv_root = 1.0 / math.sqrt(HD)
    window_rows = 3 * TILE_T * TILE_H * 3 * TILE_W

    def one_pair(pair_index):
        tile_index = pair_index // heads_here
        head_index = pair_index % heads_here
        lon_shift = tile_offsets[tile_index, 0]
        window = lax.dynamic_slice(
            extended,
            start_at(tile_index, 0, 0, 0, (lon_shift + 1) * TILE_W, head_index * HD),
            (3, 2, TILE_T, TILE_H, 3 * TILE_W, HD),
        )
        key_rows = window[:, 0].reshape(window_rows, HD)
        value_rows = window[:, 1].reshape(window_rows, HD)
        query_rows = lax.dynamic_slice(
            query_tiles,
            start_at(tile_index, 0, 0, 0, head_index * HD),
            (1, TILE_T, TILE_H, TILE_W, HD),
        ).reshape(tile_size, HD)
        scores = (
            lax.dot_general(
                query_rows, key_rows, (((1,), (1,)), ((), ())), preferred_element_type=jnp.float32
            )
            * inv_root
        )
        window_times = tile_first + tile_index - 1 + jnp.arange(3, dtype=jnp.int32)
        usable = (window_times >= 0) & (window_times < time_count)
        scores = jnp.where(
            usable[None, :, None], scores.reshape(tile_size, 3, window_rows // 3), -1e30
        )
        scores = scores.reshape(tile_size, window_rows)
        row_max = jnp.max(scores, axis=1, keepdims=True)
        raised = jnp.exp(scores - row_max)
        totals = jnp.sum(raised, axis=1, keepdims=True)
        weights = raised.astype(jnp.bfloat16)
        weighted = jnp.dot(weights, value_rows, preferred_element_type=jnp.float32)
        gate_part = lax.dynamic_slice(gate_rows, start_at(tile_index, head_index * HD), (1, HD))
        return (weighted / totals * gate_part).astype(jnp.bfloat16)

    results = lax.map(one_pair, jnp.arange(tiles_here * heads_here, dtype=jnp.int32))
    results = results.reshape(tiles_here, heads_here, TILE_T, TILE_H, TILE_W, HD)
    results = jnp.transpose(results, (0, 2, 3, 4, 1, 5))
    return results.reshape(tiles_here * TILE_T, TILE_H, TILE_W, features)


def solution(mesh):
    local = local_loop_of_four if mesh.shape["lon"] == 4 else local_any_loop
    return jax.shard_map(
        local,
        mesh=mesh,
        in_specs=(
            P("tm", None, "lon", "head"),
            P("tm", None, "lon", "head"),
            P("tm", None, "lon", "head"),
            P("tm", "lon"),
            P("tm"),
            P(None, "head"),
        ),
        out_specs=P("tm", None, "lon", "head"),
        check_vma=False,
    )
```

```python
import functools
import math

import jax
import jax.numpy as jnp
from jax import lax
from jax.experimental import pallas as pl
from jax.experimental.pallas import tpu as pltpu
from jax.sharding import PartitionSpec as P

HD = 128
FREQ = 256
TILE_T = 6
TILE_H = 8
TILE_W = 8
TILE = TILE_T * TILE_H * TILE_W
SCALE2 = math.log2(math.e) / math.sqrt(HD)
BIG = 1e30
MESH = pl.DeviceIdType.MESH
OWN, VISIT = 0, 1
LON, QUERY, UP, DOWN, UP2, DOWN2, BACK_LSE, BACK = range(8)


def attention_kernel(
    times,
    heads,
    offset_ref,
    key_ref,
    value_ref,
    query_ref,
    gate_ref,
    out_ref,
    kv,
    queries,
    scores,
    o_send,
    o_back,
    lse_send,
    lse_back,
    o_own,
    lse_own,
    staged,
    cap_own,
    cap_send,
    cap_visit,
    load_sem,
    send_sem,
    recv_sem,
    cap_sem,
    out_sem,
):
    me = lax.axis_index("lon")
    partner = me + 1 - 2 * (me % 2)
    across = 3 - me
    place = lax.axis_index("tm")
    last = lax.axis_size("tm") - 1
    has_before, has_after = place > 0, place < last
    end = times + 1

    def lanes_of(h):
        return pl.ds(pl.multiple_of(h * HD, HD), HD)

    def loads(h, picked=(0, 1, 2)):
        inner = pl.ds(1, times)
        pairs = [
            (key_ref, kv.at[h, 0, 0, inner]),
            (value_ref, kv.at[h, 0, 1, inner]),
            (query_ref, queries.at[h, OWN]),
        ]
        return [
            pltpu.make_async_copy(pairs[i][0].at[:, :, lanes_of(h)], pairs[i][1], load_sem.at[i, h])
            for i in picked
        ]

    def remote(kind, h, source, target, device):
        return pltpu.make_async_remote_copy(
            src_ref=source,
            dst_ref=target,
            send_sem=send_sem.at[kind, h],
            recv_sem=recv_sem.at[kind, h],
            device_id=device,
            device_id_type=MESH,
        )

    def lon_copy(h):
        inner = pl.ds(1, times)
        return remote(LON, h, kv.at[h, 0, :, inner], kv.at[h, 1, :, inner], {"lon": partner})

    def query_copy(h):
        return remote(QUERY, h, queries.at[h, OWN], queries.at[h, VISIT], {"lon": across})

    def up_copy(h, c):
        return remote((UP, UP2)[c], h, kv.at[h, c, :, times], kv.at[h, c, :, 0], {"tm": place + 1})

    def down_copy(h, c):
        return remote((DOWN, DOWN2)[c], h, kv.at[h, c, :, 1], kv.at[h, c, :, end], {"tm": place - 1})

    def back_copy(h, t):
        return remote(BACK + t, h, o_send.at[h, t], o_back.at[h, t], {"lon": across})

    def back_lse_copy(h):
        return remote(BACK_LSE, h, lse_send.at[h], lse_back.at[h], {"lon": across})

    def out_copy(h):
        return pltpu.make_async_copy(staged.at[h], out_ref.at[:, :, lanes_of(h)], out_sem.at[h])

    cap_copy = pltpu.make_async_remote_copy(
        src_ref=cap_send,
        dst_ref=cap_visit,
        send_sem=cap_sem.at[0],
        recv_sem=cap_sem.at[1],
        device_id={"lon": across},
        device_id_type=MESH,
    )

    def load_all(h, carry):
        for copy in loads(h):
            copy.start()
        return carry

    lax.fori_loop(0, heads, load_all, 0)

    barrier = pltpu.get_barrier_semaphore()
    for neighbour in (partner, across):
        pl.semaphore_signal(barrier, inc=1, device_id={"lon": neighbour}, device_id_type=MESH)

    @pl.when(has_before)
    def _():
        pl.semaphore_signal(barrier, inc=1, device_id={"tm": place - 1}, device_id_type=MESH)

    @pl.when(has_after)
    def _():
        pl.semaphore_signal(barrier, inc=1, device_id={"tm": place + 1}, device_id_type=MESH)

    cap_own[...] = jnp.full_like(cap_own, BIG)
    cap_send[...] = jnp.full_like(cap_send, BIG)
    across_partner = across + 1 - 2 * (across % 2)
    for t in range(times):
        shift = offset_ref[t, 0]

        def cap(column):
            return jnp.where(lax.rem(column - me - shift + 8, 4) == 2, -BIG, BIG)

        cap_own[2 * t + 1 : 2 * t + 2] = jnp.full((1, HD), cap(partner), jnp.float32)
        cap_send[2 * t : 2 * t + 1] = jnp.full((1, HD), cap(across), jnp.float32)
        cap_send[2 * t + 1 : 2 * t + 2] = jnp.full((1, HD), cap(across_partner), jnp.float32)

    def blank(slot):
        def step(h, carry):
            for c in range(2):
                for i in range(2):
                    kv[h, c, i, slot] = jnp.zeros((TILE, HD), jnp.bfloat16)
            return carry

        lax.fori_loop(0, heads, step, 0)

    @pl.when(jnp.logical_not(has_before))
    def _():
        blank(0)

    @pl.when(jnp.logical_not(has_after))
    def _():
        blank(end)

    pl.semaphore_wait(barrier, 2 + has_before.astype(jnp.int32) + has_after.astype(jnp.int32))
    cap_copy.start()

    inner = (me == 1) | (me == 2)

    def wait_queries(h, carry):
        loads(h, (2,))[0].wait()
        return carry

    def send_first(h):
        for copy in loads(h, (0, 1)):
            copy.wait()
        lon_copy(h).start()

        @pl.when(jnp.logical_not(inner))
        def _():
            query_copy(h).start()

        @pl.when(inner & (h + 2 < heads))
        def _():
            query_copy(h + 2).start()

        @pl.when(has_after)
        def _():
            up_copy(h, 0).start()

        @pl.when(has_before)
        def _():
            down_copy(h, 0).start()

    def forward(h):
        lon_copy(h).wait_recv()

        @pl.when(has_after)
        def _():
            up_copy(h, 1).start()

        @pl.when(has_before)
        def _():
            down_copy(h, 1).start()

    lax.fori_loop(0, heads, wait_queries, 0)

    @pl.when(inner)
    def _():
        query_copy(0).start()
        query_copy(1).start()

    send_first(0)
    cap_copy.wait()
    forward(0)
    send_first(1)

    before_cap = jnp.where(has_before, BIG, -BIG)
    after_cap = jnp.where(has_after, BIG, -BIG)
    ones = jnp.ones((6 * TILE, HD), jnp.bfloat16)
    wins = [(c, w) for c in range(2) for w in range(3)]

    def window(h, kind, t):
        return jnp.concatenate([kv[h, c, kind, t + w] for c, w in wins], axis=0)

    def score(h, whose, t, slot):
        scaled = queries[h, whose, t].astype(jnp.float32) * SCALE2
        high = scaled.astype(jnp.bfloat16)
        low = (scaled - high.astype(jnp.float32)).astype(jnp.bfloat16)
        query = jnp.concatenate([high, low], axis=1)
        keys = window(h, 0, t)
        scores[slot] = lax.dot_general(
            query,
            jnp.concatenate([keys, keys], axis=1),
            (((1,), (1,)), ((), ())),
            preferred_element_type=jnp.float32,
        )

    def attend(h, whose, t, slot):
        cap_ref = cap_visit if whose == VISIT else cap_own
        caps, tops = [], []
        for i, (c, w) in enumerate(wins):
            limit = cap_ref[2 * t + c : 2 * t + c + 1]
            if t + w == 0:
                limit = jnp.minimum(limit, before_cap)
            if t + w == end:
                limit = jnp.minimum(limit, after_cap)
            caps.append(limit)
            part = [
                scores[slot, :, i * TILE + j * HD : i * TILE + (j + 1) * HD] for j in range(TILE // HD)
            ]
            tops.append(jnp.minimum(functools.reduce(jnp.maximum, part), limit))
        top = jnp.max(functools.reduce(jnp.maximum, tops), axis=1, keepdims=True)
        weights = []
        for i in range(len(wins)):
            base = jnp.maximum(top, -caps[i])
            base = jnp.concatenate([base] * (TILE // HD), axis=1)
            raised = jnp.exp2(scores[slot, :, i * TILE : (i + 1) * TILE] - base)
            weights.append(raised.astype(jnp.bfloat16))
        total = jnp.dot(
            jnp.concatenate(weights, axis=1),
            jnp.concatenate([window(h, 1, t), ones], axis=1),
            preferred_element_type=jnp.float32,
        )
        sums = total[:, HD:]
        return total[:, :HD] / sums, top + jnp.log2(sums)

    def combine(h):
        for t in range(times):
            back_copy(h, t).wait_recv()
        back_lse_copy(h).wait_recv()
        pad = jnp.zeros((HD - times, TILE), jnp.float32)
        returned = jnp.transpose(jnp.concatenate([lse_back[h], pad], axis=0))
        slot = h % 2
        for t in range(times):
            mine = lse_own[slot, t]
            theirs = jnp.broadcast_to(returned[:, t : t + 1], mine.shape)
            top = jnp.maximum(mine, theirs)
            mine, theirs = jnp.exp2(mine - top), jnp.exp2(theirs - top)
            gate = gate_ref[t : t + 1, lanes_of(h)]
            mixed = o_own[slot, t] * mine + o_back[h, t].astype(jnp.float32) * theirs
            staged[h, t] = (mixed / (mine + theirs) * gate).astype(jnp.bfloat16)
        out_copy(h).start()

    first_lane = lax.broadcasted_iota(jnp.int32, (TILE, HD), 1) == 0

    def step(h, carry):
        query_copy(h).wait_recv()

        @pl.when(has_before)
        def _():
            up_copy(h, 0).wait_recv()
            up_copy(h, 1).wait_recv()

        @pl.when(has_after)
        def _():
            down_copy(h, 0).wait_recv()
            down_copy(h, 1).wait_recv()

        slot = h % 2
        score(h, VISIT, 0, 0)
        score(h, VISIT, 1, 1)
        o0, lse0 = attend(h, VISIT, 0, 0)
        o_send[h, 0] = o0.astype(jnp.bfloat16)
        back_copy(h, 0).start()
        score(h, OWN, 0, 0)
        o1, lse1 = attend(h, VISIT, 1, 1)
        o_send[h, 1] = o1.astype(jnp.bfloat16)
        lse_send[h] = jnp.transpose(jnp.where(first_lane, lse0, lse1))[:times]
        back_copy(h, 1).start()
        back_lse_copy(h).start()

        @pl.when(h + 1 < heads)
        def _():
            forward(h + 1)

        @pl.when(h + 2 < heads)
        def _():
            send_first(h + 2)

        score(h, OWN, 1, 1)
        for t in range(times):
            o, lse = attend(h, OWN, t, t)
            o_own[slot, t] = o
            lse_own[slot, t] = lse

        @pl.when(h > 0)
        def _():
            combine(h - 1)

        return carry

    lax.fori_loop(0, heads, step, 0)
    combine(heads - 1)

    def finish(h, carry):
        out_copy(h).wait()
        backs = [back_copy(h, t) for t in range(times)]
        for copy in (lon_copy(h), query_copy(h), back_lse_copy(h), *backs):
            copy.wait_send()

        @pl.when(has_after)
        def _():
            up_copy(h, 0).wait_send()
            up_copy(h, 1).wait_send()

        @pl.when(has_before)
        def _():
            down_copy(h, 0).wait_send()
            down_copy(h, 1).wait_send()

        return carry

    lax.fori_loop(0, heads, finish, 0)


def gate_of(timesteps, gate_weight):
    half_freq = FREQ // 2
    frequencies = jnp.exp(-math.log(10000.0) * jnp.arange(half_freq, dtype=jnp.float32) / half_freq)
    angles = timesteps.astype(jnp.float32)[:, None] * frequencies[None, :]
    embedding = jnp.concatenate([jnp.cos(angles), jnp.sin(angles)], axis=1)
    return jnp.dot(
        embedding, gate_weight, precision=lax.Precision.HIGHEST, preferred_element_type=jnp.float32
    )


def local_loop_of_four(query_field, key_field, value_field, tile_offsets, timesteps, gate_weight):
    times = query_field.shape[0] // TILE_T
    features = query_field.shape[3]
    heads = features // HD
    tiled = (times, TILE, features)
    query, key, value = (x.reshape(tiled) for x in (query_field, key_field, value_field))
    work = heads * times * 12 * TILE * TILE
    per_head = (heads, times, TILE, HD)
    result = pl.pallas_call(
        functools.partial(attention_kernel, times, heads),
        out_shape=jax.ShapeDtypeStruct(tiled, jnp.bfloat16),
        in_specs=[
            pl.BlockSpec(memory_space=pltpu.SMEM),
            pl.BlockSpec(memory_space=pl.ANY),
            pl.BlockSpec(memory_space=pl.ANY),
            pl.BlockSpec(memory_space=pl.ANY),
            pl.BlockSpec(memory_space=pltpu.VMEM),
        ],
        out_specs=pl.BlockSpec(memory_space=pl.ANY),
        scratch_shapes=[
            pltpu.VMEM((heads, 2, 2, times + 2, TILE, HD), jnp.bfloat16),
            pltpu.VMEM((heads, 2, times, TILE, HD), jnp.bfloat16),
            pltpu.VMEM((2, TILE, 6 * TILE), jnp.float32),
            pltpu.VMEM(per_head, jnp.bfloat16),
            pltpu.VMEM(per_head, jnp.bfloat16),
            pltpu.VMEM((heads, times, TILE), jnp.float32),
            pltpu.VMEM((heads, times, TILE), jnp.float32),
            pltpu.VMEM((2, times, TILE, HD), jnp.float32),
            pltpu.VMEM((2, times, TILE, HD), jnp.float32),
            pltpu.VMEM(per_head, jnp.bfloat16),
            pltpu.VMEM((8, HD), jnp.float32),
            pltpu.VMEM((8, HD), jnp.float32),
            pltpu.VMEM((8, HD), jnp.float32),
            pltpu.SemaphoreType.DMA((3, heads)),
            pltpu.SemaphoreType.DMA((7 + times, heads)),
            pltpu.SemaphoreType.DMA((7 + times, heads)),
            pltpu.SemaphoreType.DMA((2,)),
            pltpu.SemaphoreType.DMA((heads,)),
        ],
        compiler_params=pltpu.CompilerParams(
            collective_id=0, has_side_effects=True, vmem_limit_bytes=52 * 1024 * 1024
        ),
        cost_estimate=pl.CostEstimate(
            flops=work * 4 * HD, bytes_accessed=8 * query.size, transcendentals=work
        ),
    )(tile_offsets, key, value, query, gate_of(timesteps, gate_weight))
    return result.reshape(query_field.shape)


def from_behind(block, axis, distance):
    devices = range(lax.axis_size(axis))
    route = [((i - distance) % len(devices), i) for i in devices]
    return lax.ppermute(block, axis, route)


def extended_2(x, sides, width):
    for axis, dim in sides:
        size, length = (lax.axis_size(axis), x.shape[dim])
        up = [(i, (i + 1) % size) for i in range(size - 1)]
        down = [(j, i) for i, j in up]
        last = lax.slice_in_dim(x, length - width, length, axis=dim)
        leading = lax.slice_in_dim(x, 0, width, axis=dim)
        before = lax.ppermute(last, axis, up)
        after = lax.ppermute(leading, axis, down)
        x = jnp.concatenate([before, x, after], axis=dim)
    return x


def start_at(*entries):
    return tuple((jnp.asarray(entry).astype(jnp.int32) for entry in entries))


def lon_extend(column_block):
    pieces = {}
    for shift_by in (2, 1, -1, -2):
        pieces[shift_by] = from_behind(column_block, "lon", shift_by)
    return jnp.concatenate([pieces[2], pieces[1], column_block, pieces[-1], pieces[-2]], axis=4)


def local_any_loop(query_field, key_field, value_field, tile_offsets, timesteps, gate_weight):
    tiles_here = query_field.shape[0] // TILE_T
    features = query_field.shape[3]
    heads_here = features // HD
    tile_size = TILE_T * TILE_H * TILE_W
    tile_first = lax.axis_index("tm") * tiles_here
    time_count = tiles_here * lax.axis_size("tm")
    tiled_shape = (tiles_here, TILE_T, TILE_H, TILE_W, features)
    stacked = jnp.stack([key_field.reshape(tiled_shape), value_field.reshape(tiled_shape)], axis=1)
    rimmed = extended_2(stacked, (("tm", 0),), 1)
    extended = lon_extend(rimmed)
    half_freq = FREQ // 2
    frequencies = jnp.exp(-math.log(10000.0) * jnp.arange(half_freq, dtype=jnp.float32) / half_freq)
    angles = timesteps.astype(jnp.float32)[:, None] * frequencies[None, :]
    embedding = jnp.concatenate([jnp.cos(angles), jnp.sin(angles)], axis=1)
    gate_rows = jnp.dot(
        embedding, gate_weight, precision=lax.Precision.HIGHEST, preferred_element_type=jnp.float32
    )
    query_tiles = query_field.reshape(tiled_shape)
    inv_root = 1.0 / math.sqrt(HD)
    window_rows = 3 * TILE_T * TILE_H * 3 * TILE_W

    def one_pair(pair_index):
        tile_index = pair_index // heads_here
        head_index = pair_index % heads_here
        lon_shift = tile_offsets[tile_index, 0]
        window = lax.dynamic_slice(
            extended,
            start_at(tile_index, 0, 0, 0, (lon_shift + 1) * TILE_W, head_index * HD),
            (3, 2, TILE_T, TILE_H, 3 * TILE_W, HD),
        )
        key_rows = window[:, 0].reshape(window_rows, HD)
        value_rows = window[:, 1].reshape(window_rows, HD)
        query_rows = lax.dynamic_slice(
            query_tiles,
            start_at(tile_index, 0, 0, 0, head_index * HD),
            (1, TILE_T, TILE_H, TILE_W, HD),
        ).reshape(tile_size, HD)
        scores = (
            lax.dot_general(
                query_rows, key_rows, (((1,), (1,)), ((), ())), preferred_element_type=jnp.float32
            )
            * inv_root
        )
        window_times = tile_first + tile_index - 1 + jnp.arange(3, dtype=jnp.int32)
        usable = (window_times >= 0) & (window_times < time_count)
        scores = jnp.where(
            usable[None, :, None], scores.reshape(tile_size, 3, window_rows // 3), -1e30
        )
        scores = scores.reshape(tile_size, window_rows)
        row_max = jnp.max(scores, axis=1, keepdims=True)
        raised = jnp.exp(scores - row_max)
        totals = jnp.sum(raised, axis=1, keepdims=True)
        weights = raised.astype(jnp.bfloat16)
        weighted = jnp.dot(weights, value_rows, preferred_element_type=jnp.float32)
        gate_part = lax.dynamic_slice(gate_rows, start_at(tile_index, head_index * HD), (1, HD))
        return (weighted / totals * gate_part).astype(jnp.bfloat16)

    results = lax.map(one_pair, jnp.arange(tiles_here * heads_here, dtype=jnp.int32))
    results = results.reshape(tiles_here, heads_here, TILE_T, TILE_H, TILE_W, HD)
    results = jnp.transpose(results, (0, 2, 3, 4, 1, 5))
    return results.reshape(tiles_here * TILE_T, TILE_H, TILE_W, features)


def solution(mesh):
    local = local_loop_of_four if mesh.shape["lon"] == 4 else local_any_loop
    return jax.shard_map(
        local,
        mesh=mesh,
        in_specs=(
            P("tm", None, "lon", "head"),
            P("tm", None, "lon", "head"),
            P("tm", None, "lon", "head"),
            P("tm", "lon"),
            P("tm"),
            P(None, "head"),
        ),
        out_specs=P("tm", None, "lon", "head"),
        check_vma=False,
    )
```

```python
import functools
import math

import jax
import jax.numpy as jnp
from jax import lax
from jax.experimental import pallas as pl
from jax.experimental.pallas import tpu as pltpu
from jax.sharding import PartitionSpec as P

HD = 128
FREQ = 256
TILE_T = 6
TILE_H = 8
TILE_W = 8
TILE = TILE_T * TILE_H * TILE_W
SCALE2 = math.log2(math.e) / math.sqrt(HD)
BIG = 1e30
MESH = pl.DeviceIdType.MESH
OWN, VISIT = 0, 1
LON, UP, DOWN, UP2, DOWN2, QUERY, BACK_LSE, BACK = 0, 1, 2, 3, 4, 5, 7, 9


def attention_kernel(
    times,
    heads,
    offset_ref,
    key_ref,
    value_ref,
    query_ref,
    gate_ref,
    out_ref,
    kv,
    queries,
    scores,
    o_send,
    o_back,
    lse_send,
    lse_back,
    o_own,
    lse_own,
    staged,
    cap_own,
    cap_send,
    cap_visit,
    load_sem,
    send_sem,
    recv_sem,
    cap_sem,
    out_sem,
):
    me = lax.axis_index("lon")
    partner = me + 1 - 2 * (me % 2)
    inner = (me == 1) | (me == 2)
    guest = 1 - inner.astype(jnp.int32)
    hub = jnp.where(me < 2, 2, 1)
    hub_partner = jnp.where(me < 2, 3, 0)
    place = lax.axis_index("tm")
    last = lax.axis_size("tm") - 1
    has_before, has_after = place > 0, place < last
    end = times + 1

    def lanes_of(h):
        return pl.ds(pl.multiple_of(h * HD, HD), HD)

    def loads(h, picked=(0, 1, 2)):
        inner = pl.ds(1, times)
        pairs = [
            (key_ref, kv.at[h, 0, 0, inner]),
            (value_ref, kv.at[h, 0, 1, inner]),
            (query_ref, queries.at[h, OWN]),
        ]
        return [
            pltpu.make_async_copy(pairs[i][0].at[:, :, lanes_of(h)], pairs[i][1], load_sem.at[i, h])
            for i in picked
        ]

    def remote(kind, h, source, target, device):
        return pltpu.make_async_remote_copy(
            src_ref=source,
            dst_ref=target,
            send_sem=send_sem.at[kind, h],
            recv_sem=recv_sem.at[kind, h],
            device_id=device,
            device_id_type=MESH,
        )

    def lon_copy(h):
        inner = pl.ds(1, times)
        return remote(LON, h, kv.at[h, 0, :, inner], kv.at[h, 1, :, inner], {"lon": partner})

    def query_copy(h):
        return remote(QUERY + guest, h, queries.at[h, OWN], queries.at[h, VISIT + guest], {"lon": hub})

    def query_arrival(h, v):
        return remote(QUERY + v, h, queries.at[h, OWN], queries.at[h, VISIT + v], {"lon": hub})

    def up_copy(h, c):
        return remote((UP, UP2)[c], h, kv.at[h, c, :, times], kv.at[h, c, :, 0], {"tm": place + 1})

    def down_copy(h, c):
        return remote((DOWN, DOWN2)[c], h, kv.at[h, c, :, 1], kv.at[h, c, :, end], {"tm": place - 1})

    def visitor(v):
        return {"lon": (hub, hub_partner)[v]}

    def back_copy(h, t, v):
        return remote(BACK + times * v + t, h, o_send.at[h, v, t], o_back.at[h, t], visitor(v))

    def back_lse_copy(h, v):
        return remote(BACK_LSE + v, h, lse_send.at[h, v], lse_back.at[h], visitor(v))

    def back_arrivals(h):
        own_hub = {"lon": hub}
        return [
            remote(BACK_LSE + guest, h, lse_send.at[h, 0], lse_back.at[h], own_hub),
            *[
                remote(BACK + times * guest + t, h, o_send.at[h, 0, t], o_back.at[h, t], own_hub)
                for t in range(times)
            ],
        ]

    def out_copy(h):
        return pltpu.make_async_copy(staged.at[h], out_ref.at[:, :, lanes_of(h)], out_sem.at[h])

    def cap_copy(v):
        return pltpu.make_async_remote_copy(
            src_ref=cap_send,
            dst_ref=cap_visit.at[v],
            send_sem=cap_sem.at[0, v],
            recv_sem=cap_sem.at[1, v],
            device_id={"lon": hub},
            device_id_type=MESH,
        )

    def load_all(h, carry):
        for copy in loads(h):
            copy.start()
        return carry

    lax.fori_loop(0, heads, load_all, 0)

    barrier = pltpu.get_barrier_semaphore()
    for neighbour in (partner, hub):
        pl.semaphore_signal(barrier, inc=1, device_id={"lon": neighbour}, device_id_type=MESH)

    @pl.when(inner)
    def _():
        pl.semaphore_signal(barrier, inc=1, device_id={"lon": hub_partner}, device_id_type=MESH)

    @pl.when(has_before)
    def _():
        pl.semaphore_signal(barrier, inc=1, device_id={"tm": place - 1}, device_id_type=MESH)

    @pl.when(has_after)
    def _():
        pl.semaphore_signal(barrier, inc=1, device_id={"tm": place + 1}, device_id_type=MESH)

    cap_own[...] = jnp.full_like(cap_own, BIG)
    cap_send[...] = jnp.full_like(cap_send, BIG)
    for t in range(times):
        shift = offset_ref[t, 0]

        def cap(column):
            return jnp.where(lax.rem(column - me - shift + 8, 4) == 2, -BIG, BIG)

        cap_own[2 * t + 1 : 2 * t + 2] = jnp.full((1, HD), cap(partner), jnp.float32)
        cap_send[2 * t : 2 * t + 1] = jnp.full((1, HD), cap(hub), jnp.float32)
        cap_send[2 * t + 1 : 2 * t + 2] = jnp.full((1, HD), cap(hub_partner), jnp.float32)

    def blank(slot):
        def step(h, carry):
            for c in range(2):
                for i in range(2):
                    kv[h, c, i, slot] = jnp.zeros((TILE, HD), jnp.bfloat16)
            return carry

        lax.fori_loop(0, heads, step, 0)

    @pl.when(jnp.logical_not(has_before))
    def _():
        blank(0)

    @pl.when(jnp.logical_not(has_after))
    def _():
        blank(end)

    neighbours = 2 + inner.astype(jnp.int32) + has_before.astype(jnp.int32) + has_after.astype(jnp.int32)
    pl.semaphore_wait(barrier, neighbours)
    cap_copy(guest).start()

    def wait_queries(h, carry):
        loads(h, (2,))[0].wait()
        return carry

    def send_first(h):
        for copy in loads(h, (0, 1)):
            copy.wait()
        lon_copy(h).start()

        @pl.when(jnp.logical_not(inner))
        def _():
            query_copy(h).start()

        @pl.when(inner & (h + 3 < heads))
        def _():
            query_copy(h + 3).start()

        @pl.when(has_after)
        def _():
            up_copy(h, 0).start()

        @pl.when(has_before)
        def _():
            down_copy(h, 0).start()

    def forward(h):
        lon_copy(h).wait_recv()

        @pl.when(has_after)
        def _():
            up_copy(h, 1).start()

        @pl.when(has_before)
        def _():
            down_copy(h, 1).start()

    lax.fori_loop(0, heads, wait_queries, 0)

    @pl.when(inner)
    def _():
        query_copy(0).start()
        query_copy(1).start()
        query_copy(2).start()

    send_first(0)
    cap_copy(guest).wait_send()

    @pl.when(inner)
    def _():
        for v in range(2):
            cap_copy(v).wait_recv()

    forward(0)
    send_first(1)

    before_cap = jnp.where(has_before, BIG, -BIG)
    after_cap = jnp.where(has_after, BIG, -BIG)
    ones = jnp.ones((6 * TILE, HD), jnp.bfloat16)
    wins = [(c, w) for c in range(2) for w in range(3)]

    def window(h, kind, t):
        return jnp.concatenate([kv[h, c, kind, t + w] for c, w in wins], axis=0)

    def score(h, whose, t, slot):
        scaled = queries[h, whose, t].astype(jnp.float32) * SCALE2
        high = scaled.astype(jnp.bfloat16)
        low = (scaled - high.astype(jnp.float32)).astype(jnp.bfloat16)
        query = jnp.concatenate([high, low], axis=1)
        keys = window(h, 0, t)
        scores[slot] = lax.dot_general(
            query,
            jnp.concatenate([keys, keys], axis=1),
            (((1,), (1,)), ((), ())),
            preferred_element_type=jnp.float32,
        )

    def attend(h, whose, t, slot):
        cap_ref = cap_own if whose == OWN else cap_visit.at[whose - VISIT]
        caps, tops = [], []
        for i, (c, w) in enumerate(wins):
            limit = cap_ref[2 * t + c : 2 * t + c + 1]
            if t + w == 0:
                limit = jnp.minimum(limit, before_cap)
            if t + w == end:
                limit = jnp.minimum(limit, after_cap)
            caps.append(limit)
            part = [
                scores[slot, :, i * TILE + j * HD : i * TILE + (j + 1) * HD] for j in range(TILE // HD)
            ]
            tops.append(jnp.minimum(functools.reduce(jnp.maximum, part), limit))
        top = jnp.max(functools.reduce(jnp.maximum, tops), axis=1, keepdims=True)
        weights = []
        for i in range(len(wins)):
            base = jnp.maximum(top, -caps[i])
            base = jnp.concatenate([base] * (TILE // HD), axis=1)
            raised = jnp.exp2(scores[slot, :, i * TILE : (i + 1) * TILE] - base)
            weights.append(raised.astype(jnp.bfloat16))
        total = jnp.dot(
            jnp.concatenate(weights, axis=1),
            jnp.concatenate([window(h, 1, t), ones], axis=1),
            preferred_element_type=jnp.float32,
        )
        sums = total[:, HD:]
        return total[:, :HD] / sums, top + jnp.log2(sums)

    def combine(h):
        for copy in back_arrivals(h):
            copy.wait_recv()
        pad = jnp.zeros((HD - times, TILE), jnp.float32)
        returned = jnp.transpose(jnp.concatenate([lse_back[h], pad], axis=0))
        slot = h % 2
        for t in range(times):
            mine = lse_own[slot, t]
            theirs = jnp.broadcast_to(returned[:, t : t + 1], mine.shape)
            top = jnp.maximum(mine, theirs)
            mine, theirs = jnp.exp2(mine - top), jnp.exp2(theirs - top)
            gate = gate_ref[t : t + 1, lanes_of(h)]
            mixed = o_own[slot, t] * mine + o_back[h, t].astype(jnp.float32) * theirs
            staged[h, t] = (mixed / (mine + theirs) * gate).astype(jnp.bfloat16)
        out_copy(h).start()

    first_lane = lax.broadcasted_iota(jnp.int32, (TILE, HD), 1) == 0

    def step(h, carry):
        @pl.when(has_before)
        def _():
            up_copy(h, 0).wait_recv()
            up_copy(h, 1).wait_recv()

        @pl.when(has_after)
        def _():
            down_copy(h, 0).wait_recv()
            down_copy(h, 1).wait_recv()

        slot = h % 2

        @pl.when(inner)
        def _():
            for v in range(2):
                query_arrival(h, v).wait_recv()
            units = [(v, t) for v in range(2) for t in range(times)]
            score(h, VISIT, 0, 0)
            lses = []
            for i, (v, t) in enumerate(units):
                if i + 1 < len(units):
                    score(h, VISIT + units[i + 1][0], units[i + 1][1], (i + 1) % 2)
                o, lse = attend(h, VISIT + v, t, i % 2)
                o_send[h, v, t] = o.astype(jnp.bfloat16)
                back_copy(h, t, v).start()
                lses.append(lse)
                if t == times - 1:
                    pair = jnp.where(first_lane, lses[-2], lses[-1])
                    lse_send[h, v] = jnp.transpose(pair)[:times]
                    back_lse_copy(h, v).start()

        @pl.when(h + 1 < heads)
        def _():
            forward(h + 1)

        @pl.when(h + 2 < heads)
        def _():
            send_first(h + 2)

        score(h, OWN, 0, 0)
        score(h, OWN, 1, 1)
        for t in range(times):
            o, lse = attend(h, OWN, t, t)
            o_own[slot, t] = o
            lse_own[slot, t] = lse

        @pl.when(h > 0)
        def _():
            combine(h - 1)

        return carry

    lax.fori_loop(0, heads, step, 0)
    combine(heads - 1)

    def finish(h, carry):
        out_copy(h).wait()
        for copy in (lon_copy(h), query_copy(h)):
            copy.wait_send()

        @pl.when(inner)
        def _():
            for v in range(2):
                back_lse_copy(h, v).wait_send()
                for t in range(times):
                    back_copy(h, t, v).wait_send()

        @pl.when(has_after)
        def _():
            up_copy(h, 0).wait_send()
            up_copy(h, 1).wait_send()

        @pl.when(has_before)
        def _():
            down_copy(h, 0).wait_send()
            down_copy(h, 1).wait_send()

        return carry

    lax.fori_loop(0, heads, finish, 0)


def gate_of(timesteps, gate_weight):
    half_freq = FREQ // 2
    frequencies = jnp.exp(-math.log(10000.0) * jnp.arange(half_freq, dtype=jnp.float32) / half_freq)
    angles = timesteps.astype(jnp.float32)[:, None] * frequencies[None, :]
    embedding = jnp.concatenate([jnp.cos(angles), jnp.sin(angles)], axis=1)
    return jnp.dot(
        embedding, gate_weight, precision=lax.Precision.HIGHEST, preferred_element_type=jnp.float32
    )


def local_loop_of_four(query_field, key_field, value_field, tile_offsets, timesteps, gate_weight):
    times = query_field.shape[0] // TILE_T
    features = query_field.shape[3]
    heads = features // HD
    tiled = (times, TILE, features)
    query, key, value = (x.reshape(tiled) for x in (query_field, key_field, value_field))
    work = heads * times * 12 * TILE * TILE
    per_head = (heads, times, TILE, HD)
    result = pl.pallas_call(
        functools.partial(attention_kernel, times, heads),
        out_shape=jax.ShapeDtypeStruct(tiled, jnp.bfloat16),
        in_specs=[
            pl.BlockSpec(memory_space=pltpu.SMEM),
            pl.BlockSpec(memory_space=pl.ANY),
            pl.BlockSpec(memory_space=pl.ANY),
            pl.BlockSpec(memory_space=pl.ANY),
            pl.BlockSpec(memory_space=pltpu.VMEM),
        ],
        out_specs=pl.BlockSpec(memory_space=pl.ANY),
        scratch_shapes=[
            pltpu.VMEM((heads, 2, 2, times + 2, TILE, HD), jnp.bfloat16),
            pltpu.VMEM((heads, 3, times, TILE, HD), jnp.bfloat16),
            pltpu.VMEM((2, TILE, 6 * TILE), jnp.float32),
            pltpu.VMEM((heads, 2, times, TILE, HD), jnp.bfloat16),
            pltpu.VMEM(per_head, jnp.bfloat16),
            pltpu.VMEM((heads, 2, times, TILE), jnp.float32),
            pltpu.VMEM((heads, times, TILE), jnp.float32),
            pltpu.VMEM((2, times, TILE, HD), jnp.float32),
            pltpu.VMEM((2, times, TILE, HD), jnp.float32),
            pltpu.VMEM(per_head, jnp.bfloat16),
            pltpu.VMEM((8, HD), jnp.float32),
            pltpu.VMEM((8, HD), jnp.float32),
            pltpu.VMEM((2, 8, HD), jnp.float32),
            pltpu.SemaphoreType.DMA((3, heads)),
            pltpu.SemaphoreType.DMA((9 + 2 * times, heads)),
            pltpu.SemaphoreType.DMA((9 + 2 * times, heads)),
            pltpu.SemaphoreType.DMA((2, 2)),
            pltpu.SemaphoreType.DMA((heads,)),
        ],
        compiler_params=pltpu.CompilerParams(
            collective_id=0, has_side_effects=True, vmem_limit_bytes=52 * 1024 * 1024
        ),
        cost_estimate=pl.CostEstimate(
            flops=work * 4 * HD, bytes_accessed=8 * query.size, transcendentals=work
        ),
    )(tile_offsets, key, value, query, gate_of(timesteps, gate_weight))
    return result.reshape(query_field.shape)


def from_behind(block, axis, distance):
    devices = range(lax.axis_size(axis))
    route = [((i - distance) % len(devices), i) for i in devices]
    return lax.ppermute(block, axis, route)


def extended_2(x, sides, width):
    for axis, dim in sides:
        size, length = (lax.axis_size(axis), x.shape[dim])
        up = [(i, (i + 1) % size) for i in range(size - 1)]
        down = [(j, i) for i, j in up]
        last = lax.slice_in_dim(x, length - width, length, axis=dim)
        leading = lax.slice_in_dim(x, 0, width, axis=dim)
        before = lax.ppermute(last, axis, up)
        after = lax.ppermute(leading, axis, down)
        x = jnp.concatenate([before, x, after], axis=dim)
    return x


def start_at(*entries):
    return tuple((jnp.asarray(entry).astype(jnp.int32) for entry in entries))


def lon_extend(column_block):
    pieces = {}
    for shift_by in (2, 1, -1, -2):
        pieces[shift_by] = from_behind(column_block, "lon", shift_by)
    return jnp.concatenate([pieces[2], pieces[1], column_block, pieces[-1], pieces[-2]], axis=4)


def local_any_loop(query_field, key_field, value_field, tile_offsets, timesteps, gate_weight):
    tiles_here = query_field.shape[0] // TILE_T
    features = query_field.shape[3]
    heads_here = features // HD
    tile_size = TILE_T * TILE_H * TILE_W
    tile_first = lax.axis_index("tm") * tiles_here
    time_count = tiles_here * lax.axis_size("tm")
    tiled_shape = (tiles_here, TILE_T, TILE_H, TILE_W, features)
    stacked = jnp.stack([key_field.reshape(tiled_shape), value_field.reshape(tiled_shape)], axis=1)
    rimmed = extended_2(stacked, (("tm", 0),), 1)
    extended = lon_extend(rimmed)
    half_freq = FREQ // 2
    frequencies = jnp.exp(-math.log(10000.0) * jnp.arange(half_freq, dtype=jnp.float32) / half_freq)
    angles = timesteps.astype(jnp.float32)[:, None] * frequencies[None, :]
    embedding = jnp.concatenate([jnp.cos(angles), jnp.sin(angles)], axis=1)
    gate_rows = jnp.dot(
        embedding, gate_weight, precision=lax.Precision.HIGHEST, preferred_element_type=jnp.float32
    )
    query_tiles = query_field.reshape(tiled_shape)
    inv_root = 1.0 / math.sqrt(HD)
    window_rows = 3 * TILE_T * TILE_H * 3 * TILE_W

    def one_pair(pair_index):
        tile_index = pair_index // heads_here
        head_index = pair_index % heads_here
        lon_shift = tile_offsets[tile_index, 0]
        window = lax.dynamic_slice(
            extended,
            start_at(tile_index, 0, 0, 0, (lon_shift + 1) * TILE_W, head_index * HD),
            (3, 2, TILE_T, TILE_H, 3 * TILE_W, HD),
        )
        key_rows = window[:, 0].reshape(window_rows, HD)
        value_rows = window[:, 1].reshape(window_rows, HD)
        query_rows = lax.dynamic_slice(
            query_tiles,
            start_at(tile_index, 0, 0, 0, head_index * HD),
            (1, TILE_T, TILE_H, TILE_W, HD),
        ).reshape(tile_size, HD)
        scores = (
            lax.dot_general(
                query_rows, key_rows, (((1,), (1,)), ((), ())), preferred_element_type=jnp.float32
            )
            * inv_root
        )
        window_times = tile_first + tile_index - 1 + jnp.arange(3, dtype=jnp.int32)
        usable = (window_times >= 0) & (window_times < time_count)
        scores = jnp.where(
            usable[None, :, None], scores.reshape(tile_size, 3, window_rows // 3), -1e30
        )
        scores = scores.reshape(tile_size, window_rows)
        row_max = jnp.max(scores, axis=1, keepdims=True)
        raised = jnp.exp(scores - row_max)
        totals = jnp.sum(raised, axis=1, keepdims=True)
        weights = raised.astype(jnp.bfloat16)
        weighted = jnp.dot(weights, value_rows, preferred_element_type=jnp.float32)
        gate_part = lax.dynamic_slice(gate_rows, start_at(tile_index, head_index * HD), (1, HD))
        return (weighted / totals * gate_part).astype(jnp.bfloat16)

    results = lax.map(one_pair, jnp.arange(tiles_here * heads_here, dtype=jnp.int32))
    results = results.reshape(tiles_here, heads_here, TILE_T, TILE_H, TILE_W, HD)
    results = jnp.transpose(results, (0, 2, 3, 4, 1, 5))
    return results.reshape(tiles_here * TILE_T, TILE_H, TILE_W, features)


def solution(mesh):
    local = local_loop_of_four if mesh.shape["lon"] == 4 else local_any_loop
    return jax.shard_map(
        local,
        mesh=mesh,
        in_specs=(
            P("tm", None, "lon", "head"),
            P("tm", None, "lon", "head"),
            P("tm", None, "lon", "head"),
            P("tm", "lon"),
            P("tm"),
            P(None, "head"),
        ),
        out_specs=P("tm", None, "lon", "head"),
        check_vma=False,
    )
```

```python
import functools
import math

import jax
import jax.numpy as jnp
from jax import lax
from jax.experimental import pallas as pl
from jax.experimental.pallas import tpu as pltpu
from jax.sharding import PartitionSpec as P

HD = 128
FREQ = 256
TILE_T = 6
TILE_H = 8
TILE_W = 8
TILE = TILE_T * TILE_H * TILE_W
SCALE2 = math.log2(math.e) / math.sqrt(HD)
BIG = 1e30
MESH = pl.DeviceIdType.MESH
OWN, VISIT = 0, 1
LON, UP, DOWN, UP2, DOWN2, QUERY, BACK_LSE, BACK = 0, 1, 2, 3, 4, 5, 7, 9


def attention_kernel(
    times,
    heads,
    offset_ref,
    key_ref,
    value_ref,
    query_ref,
    gate_ref,
    out_ref,
    kv,
    queries,
    scores,
    o_send,
    o_back,
    lse_send,
    lse_back,
    o_own,
    lse_own,
    staged,
    cap_own,
    cap_send,
    cap_visit,
    load_sem,
    send_sem,
    recv_sem,
    cap_sem,
    out_sem,
):
    me = lax.axis_index("lon")
    partner = me + 1 - 2 * (me % 2)
    inner = (me == 1) | (me == 2)
    guest = 1 - inner.astype(jnp.int32)
    hub = jnp.where(me < 2, 2, 1)
    hub_partner = jnp.where(me < 2, 3, 0)
    place = lax.axis_index("tm")
    last = lax.axis_size("tm") - 1
    has_before, has_after = place > 0, place < last
    end = times + 1

    def lanes_of(h):
        return pl.ds(pl.multiple_of(h * HD, HD), HD)

    def loads(h, picked=(0, 1, 2)):
        inner = pl.ds(1, times)
        pairs = [
            (key_ref, kv.at[h, 0, 0, inner]),
            (value_ref, kv.at[h, 0, 1, inner]),
            (query_ref, queries.at[h, OWN]),
        ]
        return [
            pltpu.make_async_copy(pairs[i][0].at[:, :, lanes_of(h)], pairs[i][1], load_sem.at[i, h])
            for i in picked
        ]

    def remote(kind, h, source, target, device):
        return pltpu.make_async_remote_copy(
            src_ref=source,
            dst_ref=target,
            send_sem=send_sem.at[kind, h],
            recv_sem=recv_sem.at[kind, h],
            device_id=device,
            device_id_type=MESH,
        )

    def lon_copy(h):
        inner = pl.ds(1, times)
        return remote(LON, h, kv.at[h, 0, :, inner], kv.at[h, 1, :, inner], {"lon": partner})

    def query_copy(h):
        return remote(QUERY + guest, h, queries.at[h, OWN], queries.at[h, VISIT + guest], {"lon": hub})

    def query_arrival(h, v):
        return remote(QUERY + v, h, queries.at[h, OWN], queries.at[h, VISIT + v], {"lon": hub})

    def up_copy(h, c):
        return remote((UP, UP2)[c], h, kv.at[h, c, :, times], kv.at[h, c, :, 0], {"tm": place + 1})

    def down_copy(h, c):
        return remote((DOWN, DOWN2)[c], h, kv.at[h, c, :, 1], kv.at[h, c, :, end], {"tm": place - 1})

    def visitor(v):
        return {"lon": (hub, hub_partner)[v]}

    def back_copy(h, t, v):
        return remote(BACK + times * v + t, h, o_send.at[h, v, t], o_back.at[h, t], visitor(v))

    def back_lse_copy(h, v):
        return remote(BACK_LSE + v, h, lse_send.at[h, v], lse_back.at[h], visitor(v))

    def back_arrivals(h):
        own_hub = {"lon": hub}
        return [
            remote(BACK_LSE + guest, h, lse_send.at[h, 0], lse_back.at[h], own_hub),
            *[
                remote(BACK + times * guest + t, h, o_send.at[h, 0, t], o_back.at[h, t], own_hub)
                for t in range(times)
            ],
        ]

    def out_copy(h):
        return pltpu.make_async_copy(staged.at[h], out_ref.at[:, :, lanes_of(h)], out_sem.at[h])

    def cap_copy(v):
        return pltpu.make_async_remote_copy(
            src_ref=cap_send,
            dst_ref=cap_visit.at[v],
            send_sem=cap_sem.at[0, v],
            recv_sem=cap_sem.at[1, v],
            device_id={"lon": hub},
            device_id_type=MESH,
        )

    def load_all(h, carry):
        for copy in loads(h):
            copy.start()
        return carry

    lax.fori_loop(0, heads, load_all, 0)

    barrier = pltpu.get_barrier_semaphore()
    for neighbour in (partner, hub):
        pl.semaphore_signal(barrier, inc=1, device_id={"lon": neighbour}, device_id_type=MESH)

    @pl.when(inner)
    def _():
        pl.semaphore_signal(barrier, inc=1, device_id={"lon": hub_partner}, device_id_type=MESH)

    @pl.when(has_before)
    def _():
        pl.semaphore_signal(barrier, inc=1, device_id={"tm": place - 1}, device_id_type=MESH)

    @pl.when(has_after)
    def _():
        pl.semaphore_signal(barrier, inc=1, device_id={"tm": place + 1}, device_id_type=MESH)

    cap_own[...] = jnp.full_like(cap_own, BIG)
    cap_send[...] = jnp.full_like(cap_send, BIG)
    for t in range(times):
        shift = offset_ref[t, 0]

        def cap(column):
            return jnp.where(lax.rem(column - me - shift + 8, 4) == 2, -BIG, BIG)

        cap_own[2 * t + 1 : 2 * t + 2] = jnp.full((1, HD), cap(partner), jnp.float32)
        cap_send[2 * t : 2 * t + 1] = jnp.full((1, HD), cap(hub), jnp.float32)
        cap_send[2 * t + 1 : 2 * t + 2] = jnp.full((1, HD), cap(hub_partner), jnp.float32)

    def blank(slot):
        def step(h, carry):
            for c in range(2):
                for i in range(2):
                    kv[h, c, i, slot] = jnp.zeros((TILE, HD), jnp.bfloat16)
            return carry

        lax.fori_loop(0, heads, step, 0)

    @pl.when(jnp.logical_not(has_before))
    def _():
        blank(0)

    @pl.when(jnp.logical_not(has_after))
    def _():
        blank(end)

    neighbours = 2 + inner.astype(jnp.int32) + has_before.astype(jnp.int32) + has_after.astype(jnp.int32)
    pl.semaphore_wait(barrier, neighbours)
    cap_copy(guest).start()

    def wait_queries(h, carry):
        loads(h, (2,))[0].wait()
        return carry

    def send_first(h):
        for copy in loads(h, (0, 1)):
            copy.wait()
        lon_copy(h).start()

        @pl.when(jnp.logical_not(inner))
        def _():
            query_copy(h).start()

        @pl.when(inner & (h + 3 < heads))
        def _():
            query_copy(h + 3).start()

        @pl.when(has_after)
        def _():
            up_copy(h, 0).start()

        @pl.when(has_before)
        def _():
            down_copy(h, 0).start()

    def forward(h):
        lon_copy(h).wait_recv()

        @pl.when(has_after)
        def _():
            up_copy(h, 1).start()

        @pl.when(has_before)
        def _():
            down_copy(h, 1).start()

    lax.fori_loop(0, heads, wait_queries, 0)

    @pl.when(inner)
    def _():
        query_copy(0).start()
        query_copy(1).start()
        query_copy(2).start()

    send_first(0)
    cap_copy(guest).wait_send()

    @pl.when(inner)
    def _():
        for v in range(2):
            cap_copy(v).wait_recv()

    forward(0)
    send_first(1)

    before_cap = jnp.where(has_before, BIG, -BIG)
    after_cap = jnp.where(has_after, BIG, -BIG)
    ones = jnp.ones((6 * TILE, HD), jnp.bfloat16)
    wins = [(c, w) for c in range(2) for w in range(3)]

    def window(h, kind, t):
        return jnp.concatenate([kv[h, c, kind, t + w] for c, w in wins], axis=0)

    def score(h, whose, t, slot):
        scaled = queries[h, whose, t].astype(jnp.float32) * SCALE2
        high = scaled.astype(jnp.bfloat16)
        low = (scaled - high.astype(jnp.float32)).astype(jnp.bfloat16)
        query = jnp.concatenate([high, low], axis=1)
        keys = window(h, 0, t)
        scores[slot] = lax.dot_general(
            query,
            jnp.concatenate([keys, keys], axis=1),
            (((1,), (1,)), ((), ())),
            preferred_element_type=jnp.float32,
        )

    def attend(h, whose, t, slot):
        cap_ref = cap_own if whose == OWN else cap_visit.at[whose - VISIT]
        caps, tops = [], []
        for i, (c, w) in enumerate(wins):
            limit = cap_ref[2 * t + c : 2 * t + c + 1]
            if t + w == 0:
                limit = jnp.minimum(limit, before_cap)
            if t + w == end:
                limit = jnp.minimum(limit, after_cap)
            caps.append(limit)
            part = [
                scores[slot, :, i * TILE + j * HD : i * TILE + (j + 1) * HD] for j in range(TILE // HD)
            ]
            tops.append(jnp.minimum(functools.reduce(jnp.maximum, part), limit))
        top = jnp.max(functools.reduce(jnp.maximum, tops), axis=1, keepdims=True)
        weights = []
        for i in range(len(wins)):
            base = jnp.maximum(top, -caps[i])
            base = jnp.concatenate([base] * (TILE // HD), axis=1)
            raised = jnp.exp2(scores[slot, :, i * TILE : (i + 1) * TILE] - base)
            weights.append(raised.astype(jnp.bfloat16))
        total = jnp.dot(
            jnp.concatenate(weights, axis=1),
            jnp.concatenate([window(h, 1, t), ones], axis=1),
            preferred_element_type=jnp.float32,
        )
        sums = total[:, HD:]
        return total[:, :HD] / sums, top + jnp.log2(sums)

    def combine(h):
        for copy in back_arrivals(h):
            copy.wait_recv()
        pad = jnp.zeros((HD - times, TILE), jnp.float32)
        returned = jnp.transpose(jnp.concatenate([lse_back[h], pad], axis=0))
        slot = h % 2
        for t in range(times):
            mine = lse_own[slot, t]
            theirs = jnp.broadcast_to(returned[:, t : t + 1], mine.shape)
            top = jnp.maximum(mine, theirs)
            mine, theirs = jnp.exp2(mine - top), jnp.exp2(theirs - top)
            gate = gate_ref[t : t + 1, lanes_of(h)]
            mixed = o_own[slot, t] * mine + o_back[h, t].astype(jnp.float32) * theirs
            staged[h, t] = (mixed / (mine + theirs) * gate).astype(jnp.bfloat16)
        out_copy(h).start()

    first_lane = lax.broadcasted_iota(jnp.int32, (TILE, HD), 1) == 0

    def step(h, carry):
        @pl.when(has_before)
        def _():
            up_copy(h, 0).wait_recv()
            up_copy(h, 1).wait_recv()

        @pl.when(has_after)
        def _():
            down_copy(h, 0).wait_recv()
            down_copy(h, 1).wait_recv()

        slot = h % 2

        @pl.when(inner)
        def _():
            for v in range(2):
                query_arrival(h, v).wait_recv()
            units = [(v, t) for v in (1, 0) for t in range(times)]
            score(h, VISIT + units[0][0], units[0][1], 0)
            lses = []
            for i, (v, t) in enumerate(units):
                if i + 1 < len(units):
                    score(h, VISIT + units[i + 1][0], units[i + 1][1], (i + 1) % 2)
                o, lse = attend(h, VISIT + v, t, i % 2)
                o_send[h, v, t] = o.astype(jnp.bfloat16)
                back_copy(h, t, v).start()
                lses.append(lse)
                if t == times - 1:
                    pair = jnp.where(first_lane, lses[-2], lses[-1])
                    lse_send[h, v] = jnp.transpose(pair)[:times]
                    back_lse_copy(h, v).start()

        @pl.when(h + 1 < heads)
        def _():
            forward(h + 1)

        @pl.when(h + 2 < heads)
        def _():
            send_first(h + 2)

        score(h, OWN, 0, 0)
        score(h, OWN, 1, 1)
        for t in range(times):
            o, lse = attend(h, OWN, t, t)
            o_own[slot, t] = o
            lse_own[slot, t] = lse

        @pl.when(h > 0)
        def _():
            combine(h - 1)

        return carry

    lax.fori_loop(0, heads, step, 0)
    combine(heads - 1)

    def finish(h, carry):
        out_copy(h).wait()
        for copy in (lon_copy(h), query_copy(h)):
            copy.wait_send()

        @pl.when(inner)
        def _():
            for v in range(2):
                back_lse_copy(h, v).wait_send()
                for t in range(times):
                    back_copy(h, t, v).wait_send()

        @pl.when(has_after)
        def _():
            up_copy(h, 0).wait_send()
            up_copy(h, 1).wait_send()

        @pl.when(has_before)
        def _():
            down_copy(h, 0).wait_send()
            down_copy(h, 1).wait_send()

        return carry

    lax.fori_loop(0, heads, finish, 0)


def gate_of(timesteps, gate_weight):
    half_freq = FREQ // 2
    frequencies = jnp.exp(-math.log(10000.0) * jnp.arange(half_freq, dtype=jnp.float32) / half_freq)
    angles = timesteps.astype(jnp.float32)[:, None] * frequencies[None, :]
    embedding = jnp.concatenate([jnp.cos(angles), jnp.sin(angles)], axis=1)
    return jnp.dot(
        embedding, gate_weight, precision=lax.Precision.HIGHEST, preferred_element_type=jnp.float32
    )


def local_loop_of_four(query_field, key_field, value_field, tile_offsets, timesteps, gate_weight):
    times = query_field.shape[0] // TILE_T
    features = query_field.shape[3]
    heads = features // HD
    tiled = (times, TILE, features)
    query, key, value = (x.reshape(tiled) for x in (query_field, key_field, value_field))
    work = heads * times * 12 * TILE * TILE
    per_head = (heads, times, TILE, HD)
    result = pl.pallas_call(
        functools.partial(attention_kernel, times, heads),
        out_shape=jax.ShapeDtypeStruct(tiled, jnp.bfloat16),
        in_specs=[
            pl.BlockSpec(memory_space=pltpu.SMEM),
            pl.BlockSpec(memory_space=pl.ANY),
            pl.BlockSpec(memory_space=pl.ANY),
            pl.BlockSpec(memory_space=pl.ANY),
            pl.BlockSpec(memory_space=pltpu.VMEM),
        ],
        out_specs=pl.BlockSpec(memory_space=pl.ANY),
        scratch_shapes=[
            pltpu.VMEM((heads, 2, 2, times + 2, TILE, HD), jnp.bfloat16),
            pltpu.VMEM((heads, 3, times, TILE, HD), jnp.bfloat16),
            pltpu.VMEM((2, TILE, 6 * TILE), jnp.float32),
            pltpu.VMEM((heads, 2, times, TILE, HD), jnp.bfloat16),
            pltpu.VMEM(per_head, jnp.bfloat16),
            pltpu.VMEM((heads, 2, times, TILE), jnp.float32),
            pltpu.VMEM((heads, times, TILE), jnp.float32),
            pltpu.VMEM((2, times, TILE, HD), jnp.float32),
            pltpu.VMEM((2, times, TILE, HD), jnp.float32),
            pltpu.VMEM(per_head, jnp.bfloat16),
            pltpu.VMEM((8, HD), jnp.float32),
            pltpu.VMEM((8, HD), jnp.float32),
            pltpu.VMEM((2, 8, HD), jnp.float32),
            pltpu.SemaphoreType.DMA((3, heads)),
            pltpu.SemaphoreType.DMA((9 + 2 * times, heads)),
            pltpu.SemaphoreType.DMA((9 + 2 * times, heads)),
            pltpu.SemaphoreType.DMA((2, 2)),
            pltpu.SemaphoreType.DMA((heads,)),
        ],
        compiler_params=pltpu.CompilerParams(
            collective_id=0, has_side_effects=True, vmem_limit_bytes=52 * 1024 * 1024
        ),
        cost_estimate=pl.CostEstimate(
            flops=work * 4 * HD, bytes_accessed=8 * query.size, transcendentals=work
        ),
    )(tile_offsets, key, value, query, gate_of(timesteps, gate_weight))
    return result.reshape(query_field.shape)


def from_behind(block, axis, distance):
    devices = range(lax.axis_size(axis))
    route = [((i - distance) % len(devices), i) for i in devices]
    return lax.ppermute(block, axis, route)


def extended_2(x, sides, width):
    for axis, dim in sides:
        size, length = (lax.axis_size(axis), x.shape[dim])
        up = [(i, (i + 1) % size) for i in range(size - 1)]
        down = [(j, i) for i, j in up]
        last = lax.slice_in_dim(x, length - width, length, axis=dim)
        leading = lax.slice_in_dim(x, 0, width, axis=dim)
        before = lax.ppermute(last, axis, up)
        after = lax.ppermute(leading, axis, down)
        x = jnp.concatenate([before, x, after], axis=dim)
    return x


def start_at(*entries):
    return tuple((jnp.asarray(entry).astype(jnp.int32) for entry in entries))


def lon_extend(column_block):
    pieces = {}
    for shift_by in (2, 1, -1, -2):
        pieces[shift_by] = from_behind(column_block, "lon", shift_by)
    return jnp.concatenate([pieces[2], pieces[1], column_block, pieces[-1], pieces[-2]], axis=4)


def local_any_loop(query_field, key_field, value_field, tile_offsets, timesteps, gate_weight):
    tiles_here = query_field.shape[0] // TILE_T
    features = query_field.shape[3]
    heads_here = features // HD
    tile_size = TILE_T * TILE_H * TILE_W
    tile_first = lax.axis_index("tm") * tiles_here
    time_count = tiles_here * lax.axis_size("tm")
    tiled_shape = (tiles_here, TILE_T, TILE_H, TILE_W, features)
    stacked = jnp.stack([key_field.reshape(tiled_shape), value_field.reshape(tiled_shape)], axis=1)
    rimmed = extended_2(stacked, (("tm", 0),), 1)
    extended = lon_extend(rimmed)
    half_freq = FREQ // 2
    frequencies = jnp.exp(-math.log(10000.0) * jnp.arange(half_freq, dtype=jnp.float32) / half_freq)
    angles = timesteps.astype(jnp.float32)[:, None] * frequencies[None, :]
    embedding = jnp.concatenate([jnp.cos(angles), jnp.sin(angles)], axis=1)
    gate_rows = jnp.dot(
        embedding, gate_weight, precision=lax.Precision.HIGHEST, preferred_element_type=jnp.float32
    )
    query_tiles = query_field.reshape(tiled_shape)
    inv_root = 1.0 / math.sqrt(HD)
    window_rows = 3 * TILE_T * TILE_H * 3 * TILE_W

    def one_pair(pair_index):
        tile_index = pair_index // heads_here
        head_index = pair_index % heads_here
        lon_shift = tile_offsets[tile_index, 0]
        window = lax.dynamic_slice(
            extended,
            start_at(tile_index, 0, 0, 0, (lon_shift + 1) * TILE_W, head_index * HD),
            (3, 2, TILE_T, TILE_H, 3 * TILE_W, HD),
        )
        key_rows = window[:, 0].reshape(window_rows, HD)
        value_rows = window[:, 1].reshape(window_rows, HD)
        query_rows = lax.dynamic_slice(
            query_tiles,
            start_at(tile_index, 0, 0, 0, head_index * HD),
            (1, TILE_T, TILE_H, TILE_W, HD),
        ).reshape(tile_size, HD)
        scores = (
            lax.dot_general(
                query_rows, key_rows, (((1,), (1,)), ((), ())), preferred_element_type=jnp.float32
            )
            * inv_root
        )
        window_times = tile_first + tile_index - 1 + jnp.arange(3, dtype=jnp.int32)
        usable = (window_times >= 0) & (window_times < time_count)
        scores = jnp.where(
            usable[None, :, None], scores.reshape(tile_size, 3, window_rows // 3), -1e30
        )
        scores = scores.reshape(tile_size, window_rows)
        row_max = jnp.max(scores, axis=1, keepdims=True)
        raised = jnp.exp(scores - row_max)
        totals = jnp.sum(raised, axis=1, keepdims=True)
        weights = raised.astype(jnp.bfloat16)
        weighted = jnp.dot(weights, value_rows, preferred_element_type=jnp.float32)
        gate_part = lax.dynamic_slice(gate_rows, start_at(tile_index, head_index * HD), (1, HD))
        return (weighted / totals * gate_part).astype(jnp.bfloat16)

    results = lax.map(one_pair, jnp.arange(tiles_here * heads_here, dtype=jnp.int32))
    results = results.reshape(tiles_here, heads_here, TILE_T, TILE_H, TILE_W, HD)
    results = jnp.transpose(results, (0, 2, 3, 4, 1, 5))
    return results.reshape(tiles_here * TILE_T, TILE_H, TILE_W, features)


def solution(mesh):
    local = local_loop_of_four if mesh.shape["lon"] == 4 else local_any_loop
    return jax.shard_map(
        local,
        mesh=mesh,
        in_specs=(
            P("tm", None, "lon", "head"),
            P("tm", None, "lon", "head"),
            P("tm", None, "lon", "head"),
            P("tm", "lon"),
            P("tm"),
            P(None, "head"),
        ),
        out_specs=P("tm", None, "lon", "head"),
        check_vma=False,
    )
```
